256 devices in a mesh: dp: 4 (over x), mp: 64 (over y, z, core).
Axes of the slice: x: 4, y: 4, z: 8, core: 2. Of those that a mesh axis runs over, the one named last changes fastest.
Arguments:
- grads: bfloat16 [4, 14336, 4096], P('dp', 'mp'), may hold values from -24 to 24
- errors: float32 [4, 14336, 4096], P('dp', 'mp'), may hold values from -6 to 6
- q_start: bfloat16 [14336, 32], P('mp'), may hold values from -6 to 6
Outputs:
- update: bfloat16 [14336, 4096], P('mp')
- new_errors: float32 [4, 14336, 4096], P('dp', 'mp')
- new_q: float32 [14336, 32], P('mp')
The draws below stay inside these ranges and needn't reach their ends.
All inputs are finite; a program needn't handle non-finite values.
Results may differ from the reference program's by a relative error of at most 0.0066.
Values sent between devices are 32-bit elements; how exact they have to be, the bound alone decides.
No kernel may reach another device: no remote copies, remote signals or barrier semaphores. Data moves between devices by JAX's collectives and lax.ppermute only.
A program may use at most 64 MiB of HBM per device.

```python
import jax
import jax.numpy as jnp
from jax import lax

D = 4096
FF = 14336
RANK = 32
REPLICAS = 4


def block_scale(key, dims, cuts, least, top_value):
    def one(position, parts):
        steps = jax.random.uniform(jax.random.fold_in(jax.random.fold_in(key, 6), position), (parts,), jnp.float32, least / len(cuts), top_value / len(cuts))
        return jnp.repeat(jnp.exp(steps), dims[position] // parts).reshape((-1,) + (1,) * (len(dims) - position - 1))

    loudness = one(*cuts[0])
    for cut in cuts[1:]:
        loudness = loudness * one(*cut)
    return loudness


def gaussian(key, dims, width, most, shards=(), held_as=jnp.bfloat16):
    array = jax.random.normal(key, dims, jnp.float32) * width
    if len(shards) > 0:
        array = block_scale(key, dims, shards, -0.22, 0.18) * array
    return jnp.clip(array, min=-most, max=most).astype(held_as)


def setup_inputs(seed: int = 0) -> dict:
    key_of = jax.random.split(jax.random.key(seed), 4)
    return {
        "grads": gaussian(key_of[0], (REPLICAS, FF, D), 4.0, 24.0, ((0, 4), (1, 64))),
        "errors": gaussian(key_of[1], (REPLICAS, FF, D), 1.0, 6.0, ((0, 4), (1, 64)), jnp.float32),
        "q_start": gaussian(key_of[2], (FF, RANK), 1.0, 6.0, ((0, 64),)),
    }


def reference(grads, errors, q_start):
    compensated = grads.astype(jnp.float32) + errors
    comp_low = compensated.astype(jnp.bfloat16)
    p_sum = jnp.zeros((D, RANK), jnp.float32)
    for replica in range(REPLICAS):
        p_sum = p_sum + lax.dot_general(comp_low[replica].astype(jnp.float32), q_start.astype(jnp.float32), (((0,), (0,)), ((), ())), preferred_element_type=jnp.float32)
    gram = jnp.dot(p_sum.T, p_sum, precision=lax.Precision.HIGHEST)
    lower = jnp.linalg.cholesky(gram)
    ortho = lax.linalg.triangular_solve(lower, p_sum, left_side=False, lower=True, transpose_a=True)
    ortho_low = ortho.astype(jnp.bfloat16)
    q_total = jnp.zeros((FF, RANK), jnp.float32)
    for replica in range(REPLICAS):
        q_total = q_total + jnp.dot(comp_low[replica].astype(jnp.float32), ortho_low.astype(jnp.float32), preferred_element_type=jnp.float32)
    new_q = q_total / REPLICAS
    approx = jnp.dot(new_q, ortho.T, precision=lax.Precision.HIGHEST)
    new_errors = compensated - approx[None]
    return (approx.astype(jnp.bfloat16), new_errors, new_q)
```

```python
import jax
import jax.numpy as jnp
from jax import lax
from jax.sharding import Mesh
from jax.sharding import PartitionSpec as P

X, Y, Z, C = 4, 4, 8, 2
RANK = 32
HALF = RANK // C
FEATURES = 4096
BLOCK = FEATURES // (X * Y)


def shift(array, axis, size, step):
    return lax.ppermute(array, axis, [(i, (i + step) % size) for i in range(size)])


def sum_everywhere(partial):
    core = lax.axis_index("c")
    halves = partial.reshape(C, HALF, FEATURES)
    mine = jnp.where(core == 0, halves[0], halves[1])
    other = jnp.where(core == 0, halves[1], halves[0])
    mine = mine + shift(other, "c", C, 1)
    blocks = mine.reshape(HALF, X * Y, BLOCK).transpose(1, 0, 2)
    block = jnp.sum(lax.all_to_all(blocks, ("x", "y"), 0, 0), 0)
    block = jnp.sum(lax.all_to_all(jnp.broadcast_to(block, (Z,) + block.shape), "z", 0, 0), 0)
    blocks = lax.all_to_all(jnp.broadcast_to(block, (X * Y,) + block.shape), ("x", "y"), 0, 0)
    mine = blocks.transpose(1, 0, 2).reshape(HALF, FEATURES)
    other = shift(mine, "c", C, 1)
    return jnp.concatenate([jnp.where(core == 0, mine, other), jnp.where(core == 0, other, mine)])


def shards(grads, errors, q_start):
    compensated = grads[0].astype(jnp.float32) + errors[0]
    comp_low = compensated.astype(jnp.bfloat16)
    partial_p = lax.dot_general(
        q_start, comp_low, (((0,), (0,)), ((), ())), preferred_element_type=jnp.float32
    )
    p_t = sum_everywhere(partial_p)
    gram = jnp.dot(p_t, p_t.T, precision=lax.Precision.HIGHEST)
    lower = jnp.linalg.cholesky(gram)
    ortho_t = lax.linalg.triangular_solve(lower, p_t, left_side=True, lower=True)
    ortho_low = ortho_t.astype(jnp.bfloat16)
    local_q = lax.dot_general(
        ortho_low, comp_low, (((1,), (1,)), ((), ())), preferred_element_type=jnp.float32
    )
    left, right, across = (shift(local_q, "x", X, step) for step in (1, 3, 2))
    total_q = (local_q + across) + (left + right)
    new_q = (total_q / X).T
    approx = jnp.dot(new_q, ortho_t, precision=lax.Precision.HIGHEST)
    new_errors = (compensated - approx)[None]
    return (approx.astype(jnp.bfloat16), new_errors, new_q)


def solution(mesh):
    split = Mesh(mesh.devices.reshape(X, Y, Z, C), ("x", "y", "z", "c"))
    rows = ("y", "z", "c")
    return jax.shard_map(
        shards,
        mesh=split,
        in_specs=(P("x", rows, None), P("x", rows, None), P(rows, None)),
        out_specs=(P(rows, None), P("x", rows, None), P(rows, None)),
        check_vma=False,
    )
```

```python
import jax
import jax.numpy as jnp
from jax import lax
from jax.experimental import pallas as pl
from jax.experimental.pallas import tpu as pltpu
from jax.sharding import Mesh
from jax.sharding import PartitionSpec as P

X, Y, Z, C = 4, 4, 8, 2
RANK = 32
HALF = RANK // C
ROWS = 224
PAD = 256
FEATURES = 4096
BLOCKS = X * Y
BLOCK = FEATURES // BLOCKS
CHUNKS = 8
WIDTH = FEATURES // CHUNKS
F32, BF16 = jnp.float32, jnp.bfloat16
VMEM_LIMIT = 40 * 2**20


def columns(chunk):
    return pl.ds(chunk * WIDTH, WIDTH)


def two_terms(value):
    high = value.astype(BF16)
    return high, (value - high.astype(F32)).astype(BF16)


def three_terms(value):
    high, rest = value.astype(BF16), value
    rest = value - high.astype(F32)
    middle = rest.astype(BF16)
    return high, middle, (rest - middle.astype(F32)).astype(BF16)


def compensate_kernel(
    grads, errors, q_hbm, comp, low, mine, other, grad_buf, q_t, q_sem, grad_sems, error_sems
):
    q_copy = pltpu.make_async_copy(q_hbm, q_t, q_sem)
    q_copy.start()
    copies = []
    for chunk in range(CHUNKS):
        cols = columns(chunk)
        pair = (
            pltpu.make_async_copy(grads.at[:, cols], grad_buf.at[:, cols], grad_sems.at[chunk]),
            pltpu.make_async_copy(errors.at[:, cols], comp.at[:, cols], error_sems.at[chunk]),
        )
        for copy in pair:
            copy.start()
        copies.append(pair)
    q_copy.wait()
    first = lax.axis_index("c") == 0
    top, bottom = q_t[:HALF, :], q_t[HALF:, :]
    factor = jnp.concatenate([jnp.where(first, top, bottom), jnp.where(first, bottom, top)])
    for chunk in range(CHUNKS):
        for copy in copies[chunk]:
            copy.wait()
        cols = columns(chunk)
        total = grad_buf[:, cols].astype(F32) + comp[:, cols]
        comp[:, cols] = total
        rounded = total.astype(BF16)
        low[:, cols] = rounded
        partial = jnp.dot(factor, rounded, preferred_element_type=F32)
        for part in range(WIDTH // BLOCK):
            block = chunk * (WIDTH // BLOCK) + part
            at = slice(part * BLOCK, (part + 1) * BLOCK)
            mine[block] = partial[:HALF, at]
            other[block] = partial[HALF:, at]


def compensate(grads, errors, q_t):
    vmem = pl.BlockSpec(memory_space=pltpu.VMEM)
    hbm = pl.BlockSpec(memory_space=pltpu.HBM)
    half = pltpu.VMEM((BLOCKS, HALF, BLOCK), F32)
    return pl.pallas_call(
        compensate_kernel,
        out_shape=(
            pltpu.VMEM((ROWS, FEATURES), F32),
            pltpu.VMEM((ROWS, FEATURES), BF16),
            half,
            half,
        ),
        in_specs=[hbm] * 3,
        out_specs=[vmem] * 4,
        scratch_shapes=[
            pltpu.VMEM((ROWS, FEATURES), BF16),
            pltpu.VMEM((RANK, ROWS), BF16),
            pltpu.SemaphoreType.DMA,
            pltpu.SemaphoreType.DMA((CHUNKS,)),
            pltpu.SemaphoreType.DMA((CHUNKS,)),
        ],
        compiler_params=pltpu.CompilerParams(vmem_limit_bytes=VMEM_LIMIT),
        name="compensate",
    )(
        pltpu.with_memory_space_constraint(grads, pltpu.HBM),
        pltpu.with_memory_space_constraint(errors, pltpu.HBM),
        pltpu.with_memory_space_constraint(q_t, pltpu.HBM),
    )


def project_kernel(low, mine, other, product, terms):
    core = lax.axis_index("c")
    for block in range(BLOCKS):
        for half, row in ((mine, core * HALF), (other, (1 - core) * HALF)):
            for term, value in enumerate(three_terms(half[block])):
                rows = pl.ds(pl.multiple_of(term * RANK + row, HALF), HALF)
                terms[rows, block * BLOCK : (block + 1) * BLOCK] = value
    stacked = lax.dot_general(low[...], terms[...], (((1,), (1,)), ((), ())), preferred_element_type=F32)
    total = stacked[:, :RANK] + (stacked[:, RANK : 2 * RANK] + stacked[:, 2 * RANK :])
    padded = jnp.concatenate([total, jnp.zeros((PAD - ROWS, RANK), F32)])
    product[...] = padded.T


def project(low, mine, other):
    vmem = pl.BlockSpec(memory_space=pltpu.VMEM)
    return pl.pallas_call(
        project_kernel,
        out_shape=(pltpu.VMEM((RANK, PAD), F32), pltpu.VMEM((3 * RANK, FEATURES), BF16)),
        in_specs=[vmem] * 3,
        out_specs=[vmem] * 2,
        compiler_params=pltpu.CompilerParams(vmem_limit_bytes=VMEM_LIMIT),
        name="project",
    )(pltpu.with_memory_space_constraint(low, pltpu.VMEM), mine, other)


def inverse_of_lower(gram):
    row = lax.broadcasted_iota(jnp.int32, (RANK, RANK), 0)
    column = lax.broadcasted_iota(jnp.int32, (RANK, RANK), 1)
    work = jnp.concatenate([gram, (row == column).astype(F32)], axis=1)
    index = lax.broadcasted_iota(jnp.int32, (RANK, 2 * RANK), 0)
    scale = jnp.zeros((RANK, 2 * RANK), F32)
    for step in range(RANK):
        pivot_row = jnp.broadcast_to(work[step : step + 1, :], work.shape)
        pivot = jnp.broadcast_to(work[step : step + 1, step : step + 1], work.shape)
        multiplier = jnp.broadcast_to(work[:, step : step + 1], work.shape) / pivot
        scale = jnp.where(index == step, pivot, scale)
        work = jnp.where(index > step, work - multiplier * pivot_row, work)
    return (work / jnp.sqrt(scale))[:, RANK:]


def factor_kernel(terms, inverse, ortho):
    stacked = lax.dot_general(terms[...], terms[...], (((1,), (1,)), ((), ())), preferred_element_type=F32)

    def part(left, right):
        return stacked[left * RANK : (left + 1) * RANK, right * RANK : (right + 1) * RANK]

    small = part(0, 2) + part(2, 0) + part(1, 1)
    gram = part(0, 0) + ((part(0, 1) + part(1, 0)) + small)
    lower_inverse = inverse_of_lower(gram)
    inverse[...] = lower_inverse
    for chunk in range(CHUNKS):
        cols = columns(chunk)
        p_t = (
            terms[:RANK, cols].astype(F32)
            + terms[RANK : 2 * RANK, cols].astype(F32)
            + terms[2 * RANK :, cols].astype(F32)
        )
        ortho_t = jnp.dot(
            lower_inverse, p_t, precision=lax.Precision.HIGHEST, preferred_element_type=F32
        )
        high, low = two_terms(ortho_t)
        ortho[:RANK, cols] = high
        ortho[RANK : 2 * RANK, cols] = low
        ortho[2 * RANK :, cols] = high


def factor(terms):
    vmem = pl.BlockSpec(memory_space=pltpu.VMEM)
    return pl.pallas_call(
        factor_kernel,
        out_shape=(pltpu.VMEM((RANK, RANK), F32), pltpu.VMEM((3 * RANK, FEATURES), BF16)),
        in_specs=[vmem],
        out_specs=[vmem] * 2,
        compiler_params=pltpu.CompilerParams(vmem_limit_bytes=VMEM_LIMIT),
        cost_estimate=pl.CostEstimate(flops=10**9, bytes_accessed=10**7, transcendentals=0),
        name="factor",
    )(terms)


def apply_kernel(
    comp, own, across, left, right, inverse, ortho, new_errors, update, new_q, error_buf, update_buf, error_sems, update_sems
):
    total = (own[...] + across[...]) + (left[...] + right[...])
    q_t = jnp.dot(
        inverse[...], total * (1.0 / X), precision=lax.Precision.HIGHEST, preferred_element_type=F32
    )
    new_q[...] = q_t[:, :ROWS]
    high = q_t.astype(BF16).astype(F32)
    stacked = jnp.concatenate([high, high, q_t - high]).T[:ROWS].astype(BF16)
    copies = []
    for chunk in range(CHUNKS):
        cols = columns(chunk)
        approx = jnp.dot(stacked, ortho[:, cols], preferred_element_type=F32)
        error_buf[:, cols] = comp[:, cols] - approx
        update_buf[:, cols] = approx.astype(BF16)
        copies += [
            pltpu.make_async_copy(error_buf.at[:, cols], new_errors.at[:, cols], error_sems.at[chunk]),
            pltpu.make_async_copy(update_buf.at[:, cols], update.at[:, cols], update_sems.at[chunk]),
        ]
        for copy in copies[-2:]:
            copy.start()
    for copy in copies:
        copy.wait()


def apply(comp, own, across, left, right, inverse, ortho):
    vmem = pl.BlockSpec(memory_space=pltpu.VMEM)
    hbm = pl.BlockSpec(memory_space=pl.ANY)
    return pl.pallas_call(
        apply_kernel,
        out_shape=(
            jax.ShapeDtypeStruct((ROWS, FEATURES), F32),
            jax.ShapeDtypeStruct((ROWS, FEATURES), BF16),
            jax.ShapeDtypeStruct((RANK, ROWS), F32),
        ),
        in_specs=[vmem] * 7,
        out_specs=[hbm, hbm, vmem],
        scratch_shapes=[
            pltpu.VMEM((ROWS, FEATURES), F32),
            pltpu.VMEM((ROWS, FEATURES), BF16),
            pltpu.SemaphoreType.DMA((CHUNKS,)),
            pltpu.SemaphoreType.DMA((CHUNKS,)),
        ],
        compiler_params=pltpu.CompilerParams(vmem_limit_bytes=VMEM_LIMIT),
        name="apply",
    )(pltpu.with_memory_space_constraint(comp, pltpu.VMEM), own, across, left, right, inverse, ortho)


def shift(array, axis, size, step):
    return lax.ppermute(array, axis, [(i, (i + step) % size) for i in range(size)])


def repeat(block, times):
    return jnp.broadcast_to(block, (times,) + block.shape)


def sum_everywhere(mine, other):
    mine = mine + shift(other, "c", C, 1)
    block = jnp.sum(lax.all_to_all(mine, ("x", "y"), 0, 0), 0)
    block = jnp.sum(lax.all_to_all(repeat(block, Z), "z", 0, 0), 0)
    mine = lax.all_to_all(repeat(block, BLOCKS), ("x", "y"), 0, 0)
    return mine, shift(mine, "c", C, 1)


def shards(grads, errors, q_start):
    comp, low, mine, other = compensate(grads[0], errors[0], q_start.T)
    mine, other = sum_everywhere(mine, other)
    product, terms = project(low, mine, other)
    across, left, right = (shift(product, "x", X, step) for step in (2, 1, 3))
    inverse, ortho = factor(terms)
    new_errors, update, new_q = apply(comp, product, across, left, right, inverse, ortho)
    return (update, new_errors[None], new_q.T)


def solution(mesh):
    split = Mesh(mesh.devices.reshape(X, Y, Z, C), ("x", "y", "z", "c"))
    rows = ("y", "z", "c")
    return jax.shard_map(
        shards,
        mesh=split,
        in_specs=(P("x", rows, None), P("x", rows, None), P(rows, None)),
        out_specs=(P(rows, None), P("x", rows, None), P(rows, None)),
        check_vma=False,
    )
```

```python
import jax
import jax.numpy as jnp
from jax import lax
from jax.experimental import pallas as pl
from jax.experimental.pallas import tpu as pltpu
from jax.sharding import Mesh
from jax.sharding import PartitionSpec as P

X, Y, Z, C = 4, 4, 8, 2
RANK = 32
HALF = RANK // C
ROWS = 224
PAD = 256
FEATURES = 4096
BLOCKS = X * Y
BLOCK = FEATURES // BLOCKS
CHUNKS = 4
GROUP = 8
WIDTH = FEATURES // CHUNKS
F32, BF16 = jnp.float32, jnp.bfloat16
VMEM_LIMIT = 20 * 2**20


def columns(chunk):
    return pl.ds(chunk * WIDTH, WIDTH)


def two_terms(value):
    high = value.astype(BF16)
    return high, (value - high.astype(F32)).astype(BF16)


def three_terms(value):
    high, rest = value.astype(BF16), value
    rest = value - high.astype(F32)
    middle = rest.astype(BF16)
    return high, middle, (rest - middle.astype(F32)).astype(BF16)


def compensate_kernel(
    grads, errors, q_hbm, comp, low, mine, other, grad_buf, q_t, q_sem, grad_sems, error_sems
):
    q_copy = pltpu.make_async_copy(q_hbm, q_t, q_sem)
    q_copy.start()
    copies = []
    for chunk in range(CHUNKS):
        cols = columns(chunk)
        pair = (
            pltpu.make_async_copy(grads.at[:, cols], grad_buf.at[:, cols], grad_sems.at[chunk]),
            pltpu.make_async_copy(errors.at[:, cols], comp.at[:, cols], error_sems.at[chunk]),
        )
        for copy in pair:
            copy.start()
        copies.append(pair)
    q_copy.wait()
    first = lax.axis_index("c") == 0
    top, bottom = q_t[:HALF, :], q_t[HALF:, :]
    factor = jnp.concatenate([jnp.where(first, top, bottom), jnp.where(first, bottom, top)])
    for chunk in range(CHUNKS):
        for copy in copies[chunk]:
            copy.wait()
        cols = columns(chunk)
        total = grad_buf[:, cols].astype(F32) + comp[:, cols]
        comp[:, cols] = total
        rounded = total.astype(BF16)
        low[:, cols] = rounded
        partial = jnp.dot(factor, rounded, preferred_element_type=F32)
        for part in range(WIDTH // BLOCK):
            block = chunk * (WIDTH // BLOCK) + part
            at = slice(part * BLOCK, (part + 1) * BLOCK)
            mine[block] = partial[:HALF, at]
            other[block] = partial[HALF:, at]


def compensate(grads, errors, q_t):
    vmem = pl.BlockSpec(memory_space=pltpu.VMEM)
    hbm = pl.BlockSpec(memory_space=pltpu.HBM)
    half = pltpu.VMEM((BLOCKS, HALF, BLOCK), F32)
    return pl.pallas_call(
        compensate_kernel,
        out_shape=(
            pltpu.VMEM((ROWS, FEATURES), F32),
            pltpu.VMEM((ROWS, FEATURES), BF16),
            half,
            half,
        ),
        in_specs=[hbm] * 3,
        out_specs=[vmem] * 4,
        scratch_shapes=[
            pltpu.VMEM((ROWS, FEATURES), BF16),
            pltpu.VMEM((RANK, ROWS), BF16),
            pltpu.SemaphoreType.DMA,
            pltpu.SemaphoreType.DMA((CHUNKS,)),
            pltpu.SemaphoreType.DMA((CHUNKS,)),
        ],
        compiler_params=pltpu.CompilerParams(vmem_limit_bytes=VMEM_LIMIT),
        name="compensate",
    )(
        pltpu.with_memory_space_constraint(grads, pltpu.HBM),
        pltpu.with_memory_space_constraint(errors, pltpu.HBM),
        pltpu.with_memory_space_constraint(q_t, pltpu.HBM),
    )


def project_kernel(low, mine, other, product, terms):
    core = lax.axis_index("c")
    for block in range(BLOCKS):
        for half, row in ((mine, core * HALF), (other, (1 - core) * HALF)):
            for term, value in enumerate(three_terms(half[block])):
                rows = pl.ds(pl.multiple_of(term * RANK + row, HALF), HALF)
                terms[rows, block * BLOCK : (block + 1) * BLOCK] = value
    stacked = lax.dot_general(low[...], terms[...], (((1,), (1,)), ((), ())), preferred_element_type=F32)
    total = stacked[:, :RANK] + (stacked[:, RANK : 2 * RANK] + stacked[:, 2 * RANK :])
    padded = jnp.concatenate([total, jnp.zeros((PAD - ROWS, RANK), F32)])
    product[...] = padded.T


def project(low, mine, other):
    vmem = pl.BlockSpec(memory_space=pltpu.VMEM)
    return pl.pallas_call(
        project_kernel,
        out_shape=(pltpu.VMEM((RANK, PAD), F32), pltpu.VMEM((3 * RANK, FEATURES), BF16)),
        in_specs=[vmem] * 3,
        out_specs=[vmem] * 2,
        compiler_params=pltpu.CompilerParams(vmem_limit_bytes=VMEM_LIMIT),
        name="project",
    )(pltpu.with_memory_space_constraint(low, pltpu.VMEM), mine, other)


def inverse_of_lower(gram):
    shape = (GROUP, 2 * RANK)
    groups = RANK // GROUP
    row = lax.broadcasted_iota(jnp.int32, (RANK, RANK), 0)
    column = lax.broadcasted_iota(jnp.int32, (RANK, RANK), 1)
    whole = jnp.concatenate([gram, (row == column).astype(F32)], axis=1)
    work = [whole[g * GROUP : (g + 1) * GROUP] for g in range(groups)]
    index = lax.broadcasted_iota(jnp.int32, shape, 0)
    scale = [jnp.zeros(shape, F32) for _ in range(groups)]
    inside = range(GROUP)
    for g in range(groups):
        rows = [jnp.broadcast_to(work[g][p : p + 1, :], shape) for p in inside]
        cols = [
            [jnp.broadcast_to(work[i][:, g * GROUP + p : g * GROUP + p + 1], shape) for i in range(g, groups)]
            for p in inside
        ]
        entry = {
            (q, p): jnp.broadcast_to(cols[p][0][q : q + 1, :], shape) for p in inside for q in range(p, GROUP)
        }
        for p in inside:
            reciprocal = 1.0 / entry[p, p]
            scale[g] = jnp.where(index == p, entry[p, p], scale[g])
            for q in range(p + 1, GROUP):
                multiplier = entry[q, p] * reciprocal
                for t in range(q, GROUP):
                    entry[t, q] = entry[t, q] - multiplier * entry[t, p]
                rows[q] = rows[q] - multiplier * rows[p]
                cols[q] = [mine - multiplier * pivot for mine, pivot in zip(cols[q], cols[p])]
            rows[p] = rows[p] * reciprocal
        for i in range(g, groups):
            for p in inside:
                factor = cols[p][i - g]
                if i == g:
                    factor = jnp.where(index > p, factor, 0.0)
                work[i] = work[i] - factor * rows[p]
    return jnp.concatenate([w * lax.rsqrt(d) for w, d in zip(work, scale)])[:, RANK:]


def factor_kernel(terms, inverse, ortho):
    stacked = lax.dot_general(terms[...], terms[...], (((1,), (1,)), ((), ())), preferred_element_type=F32)

    def part(left, right):
        return stacked[left * RANK : (left + 1) * RANK, right * RANK : (right + 1) * RANK]

    small = part(0, 2) + part(2, 0) + part(1, 1)
    gram = part(0, 0) + ((part(0, 1) + part(1, 0)) + small)
    lower_inverse = inverse_of_lower(gram)
    inverse[...] = lower_inverse
    for chunk in range(CHUNKS):
        cols = columns(chunk)
        p_t = (
            terms[:RANK, cols].astype(F32)
            + terms[RANK : 2 * RANK, cols].astype(F32)
            + terms[2 * RANK :, cols].astype(F32)
        )
        ortho_t = jnp.dot(
            lower_inverse, p_t, precision=lax.Precision.HIGHEST, preferred_element_type=F32
        )
        high, low = two_terms(ortho_t)
        ortho[:RANK, cols] = high
        ortho[RANK : 2 * RANK, cols] = low
        ortho[2 * RANK :, cols] = high


def factor(terms):
    vmem = pl.BlockSpec(memory_space=pltpu.VMEM)
    return pl.pallas_call(
        factor_kernel,
        out_shape=(pltpu.VMEM((RANK, RANK), F32), pltpu.VMEM((3 * RANK, FEATURES), BF16)),
        in_specs=[vmem],
        out_specs=[vmem] * 2,
        compiler_params=pltpu.CompilerParams(vmem_limit_bytes=VMEM_LIMIT),
        cost_estimate=pl.CostEstimate(flops=10**9, bytes_accessed=10**7, transcendentals=0),
        name="factor",
    )(terms)


def apply_kernel(
    comp, own, across, left, right, inverse, ortho, new_errors, update, new_q, error_buf, update_buf, error_sems, update_sems
):
    total = (own[...] + across[...]) + (left[...] + right[...])
    q_t = jnp.dot(
        inverse[...], total * (1.0 / X), precision=lax.Precision.HIGHEST, preferred_element_type=F32
    )
    new_q[...] = q_t[:, :ROWS]
    high = q_t.astype(BF16).astype(F32)
    stacked = jnp.concatenate([high, high, q_t - high]).T[:ROWS].astype(BF16)
    copies = []
    for chunk in range(CHUNKS):
        cols = columns(chunk)
        approx = jnp.dot(stacked, ortho[:, cols], preferred_element_type=F32)
        error_buf[:, cols] = comp[:, cols] - approx
        update_buf[:, cols] = approx.astype(BF16)
        copies += [
            pltpu.make_async_copy(error_buf.at[:, cols], new_errors.at[:, cols], error_sems.at[chunk]),
            pltpu.make_async_copy(update_buf.at[:, cols], update.at[:, cols], update_sems.at[chunk]),
        ]
        for copy in copies[-2:]:
            copy.start()
    for copy in copies:
        copy.wait()


def apply(comp, own, across, left, right, inverse, ortho):
    vmem = pl.BlockSpec(memory_space=pltpu.VMEM)
    hbm = pl.BlockSpec(memory_space=pl.ANY)
    return pl.pallas_call(
        apply_kernel,
        out_shape=(
            jax.ShapeDtypeStruct((ROWS, FEATURES), F32),
            jax.ShapeDtypeStruct((ROWS, FEATURES), BF16),
            jax.ShapeDtypeStruct((RANK, ROWS), F32),
        ),
        in_specs=[vmem] * 7,
        out_specs=[hbm, hbm, vmem],
        scratch_shapes=[
            pltpu.VMEM((ROWS, FEATURES), F32),
            pltpu.VMEM((ROWS, FEATURES), BF16),
            pltpu.SemaphoreType.DMA((CHUNKS,)),
            pltpu.SemaphoreType.DMA((CHUNKS,)),
        ],
        compiler_params=pltpu.CompilerParams(vmem_limit_bytes=VMEM_LIMIT),
        name="apply",
    )(pltpu.with_memory_space_constraint(comp, pltpu.VMEM), own, across, left, right, inverse, ortho)


def shift(array, axis, size, step):
    return lax.ppermute(array, axis, [(i, (i + step) % size) for i in range(size)])


def add_up(blocks):
    terms = [blocks[i] for i in range(blocks.shape[0])]
    while len(terms) > 1:
        terms = [left + right for left, right in zip(terms[::2], terms[1::2])]
    return terms[0]


def repeat(block, times):
    return jnp.broadcast_to(block, (times,) + block.shape)


def sum_everywhere(mine, other):
    mine = mine + shift(other, "c", C, 1)
    block = add_up(lax.all_to_all(mine, ("x", "y"), 0, 0))
    block = add_up(lax.all_to_all(repeat(block, Z), "z", 0, 0))
    mine = lax.all_to_all(repeat(block, BLOCKS), ("x", "y"), 0, 0)
    return mine, shift(mine, "c", C, 1)


def shards(grads, errors, q_start):
    comp, low, mine, other = compensate(grads[0], errors[0], q_start.T)
    mine, other = sum_everywhere(mine, other)
    product, terms = project(low, mine, other)
    across, left, right = (shift(product, "x", X, step) for step in (2, 1, 3))
    inverse, ortho = factor(terms)
    new_errors, update, new_q = apply(comp, product, across, left, right, inverse, ortho)
    return (update, new_errors[None], new_q.T)


def solution(mesh):
    split = Mesh(mesh.devices.reshape(X, Y, Z, C), ("x", "y", "z", "c"))
    rows = ("y", "z", "c")
    return jax.shard_map(
        shards,
        mesh=split,
        in_specs=(P("x", rows, None), P("x", rows, None), P(rows, None)),
        out_specs=(P(rows, None), P("x", rows, None), P(rows, None)),
        check_vma=False,
    )
```

```python
import functools

import jax
import jax.numpy as jnp
from jax import lax
from jax.experimental import pallas as pl
from jax.experimental.pallas import tpu as pltpu
from jax.sharding import Mesh
from jax.sharding import PartitionSpec as P

X, Y, Z, C = 4, 4, 8, 2
RANK = 32
ROWS = 224
PAD = 256
FEATURES = 4096
HALF = FEATURES // C
BLOCKS = X * Y
BLOCK = HALF // BLOCKS
CHUNKS = 2
WIDTH = HALF // CHUNKS
GROUP = 8
F32, BF16 = jnp.float32, jnp.bfloat16
CONTRACT_LAST = (((1,), (1,)), ((), ()))
VMEM = pl.BlockSpec(memory_space=pltpu.VMEM)
HBM = pl.BlockSpec(memory_space=pltpu.HBM)


def half_start(own):
    core = lax.axis_index("c")
    return (core if own else 1 - core) * HALF


def in_hbm(start, chunk):
    return pl.ds(pl.multiple_of(start + chunk * WIDTH, WIDTH), WIDTH)


def in_half(chunk):
    return slice(chunk * WIDTH, (chunk + 1) * WIDTH)


def params(mebibytes):
    return pltpu.CompilerParams(vmem_limit_bytes=mebibytes * 2**20)


def two_terms(value):
    high = value.astype(BF16)
    return high, (value - high.astype(F32)).astype(BF16)


def three_terms(value):
    high = value.astype(BF16)
    rest = value - high.astype(F32)
    middle = rest.astype(BF16)
    return high, middle, (rest - middle.astype(F32)).astype(BF16)


def compensate_kernel(
    own, grads, errors, q_hbm, comp, low, partial, grad_buf, q_t, q_sem, grad_sems, error_sems
):
    start = half_start(own)
    copies = []
    for chunk in range(CHUNKS):
        at, cols = in_hbm(start, chunk), in_half(chunk)
        pair = (
            pltpu.make_async_copy(grads.at[:, at], grad_buf.at[:, cols], grad_sems.at[chunk]),
            pltpu.make_async_copy(errors.at[:, at], comp.at[:, cols], error_sems.at[chunk]),
        )
        for copy in pair:
            copy.start()
        copies.append(pair)
    q_copy = pltpu.make_async_copy(q_hbm, q_t, q_sem)
    q_copy.start()
    q_copy.wait()
    factor = q_t[...]
    for chunk in range(CHUNKS):
        for copy in copies[chunk]:
            copy.wait()
        cols = in_half(chunk)
        total = grad_buf[:, cols].astype(F32) + comp[:, cols]
        comp[:, cols] = total
        rounded = total.astype(BF16)
        low[:, cols] = rounded
        product = jnp.dot(factor, rounded, preferred_element_type=F32)
        for part in range(WIDTH // BLOCK):
            partial[chunk * (WIDTH // BLOCK) + part] = product[:, part * BLOCK : (part + 1) * BLOCK]


def compensate(grads, errors, q_t, own):
    operands = [pltpu.with_memory_space_constraint(a, pltpu.HBM) for a in (grads, errors, q_t)]
    return pl.pallas_call(
        functools.partial(compensate_kernel, own),
        out_shape=(
            pltpu.VMEM((ROWS, HALF), F32),
            pltpu.VMEM((ROWS, HALF), BF16),
            pltpu.VMEM((BLOCKS, RANK, BLOCK), F32),
        ),
        in_specs=[HBM] * 3,
        out_specs=[VMEM] * 3,
        scratch_shapes=[
            pltpu.VMEM((ROWS, HALF), BF16),
            pltpu.VMEM((RANK, ROWS), BF16),
            pltpu.SemaphoreType.DMA,
            pltpu.SemaphoreType.DMA((CHUNKS,)),
            pltpu.SemaphoreType.DMA((CHUNKS,)),
        ],
        compiler_params=params(12),
        cost_estimate=pl.CostEstimate(
            flops=2 * ROWS * HALF * RANK, bytes_accessed=6 * ROWS * HALF, transcendentals=0
        ),
        name="compensate_own" if own else "compensate_other",
    )(*operands)


def project_kernel(low, blocks, *refs):
    product, terms = refs[-2:]
    for block in range(BLOCKS):
        cols = slice(block * BLOCK, (block + 1) * BLOCK)
        for term, value in enumerate(three_terms(blocks[block])):
            terms[term * RANK : (term + 1) * RANK, cols] = value
    stacked = lax.dot_general(terms[...], low[...], CONTRACT_LAST, preferred_element_type=F32)
    total = stacked[:RANK] + (stacked[RANK : 2 * RANK] + stacked[2 * RANK :])
    if len(refs) == 3:
        total = total + refs[0][:, :ROWS]
    product[...] = jnp.zeros(product.shape, F32)
    product[:, :ROWS] = total


def project(low, blocks, *before):
    return pl.pallas_call(
        project_kernel,
        out_shape=(pltpu.VMEM((RANK, PAD), F32), pltpu.VMEM((3 * RANK, HALF), BF16)),
        in_specs=[VMEM] * (2 + len(before)),
        out_specs=[VMEM] * 2,
        compiler_params=params(12),
        cost_estimate=pl.CostEstimate(
            flops=6 * ROWS * HALF * RANK, bytes_accessed=2 * ROWS * HALF, transcendentals=0
        ),
        name="project",
    )(pltpu.with_memory_space_constraint(low, pltpu.VMEM), blocks, *before)


def inverse_of_lower(gram):
    shape = (GROUP, 2 * RANK)
    groups = RANK // GROUP
    row = lax.broadcasted_iota(jnp.int32, (RANK, RANK), 0)
    column = lax.broadcasted_iota(jnp.int32, (RANK, RANK), 1)
    whole = jnp.concatenate([gram, (row == column).astype(F32)], axis=1)
    work = [whole[g * GROUP : (g + 1) * GROUP] for g in range(groups)]
    index = lax.broadcasted_iota(jnp.int32, shape, 0)
    scale = [jnp.zeros(shape, F32) for _ in range(groups)]
    inside = range(GROUP)
    for g in range(groups):
        rows = [jnp.broadcast_to(work[g][p : p + 1, :], shape) for p in inside]
        cols = [
            [jnp.broadcast_to(work[i][:, g * GROUP + p : g * GROUP + p + 1], shape) for i in range(g, groups)]
            for p in inside
        ]
        entry = {
            (q, p): jnp.broadcast_to(cols[p][0][q : q + 1, :], shape) for p in inside for q in range(p, GROUP)
        }
        for p in inside:
            reciprocal = 1.0 / entry[p, p]
            scale[g] = jnp.where(index == p, entry[p, p], scale[g])
            for q in range(p + 1, GROUP):
                multiplier = entry[q, p] * reciprocal
                for t in range(q, GROUP):
                    entry[t, q] = entry[t, q] - multiplier * entry[t, p]
                rows[q] = rows[q] - multiplier * rows[p]
                cols[q] = [mine - multiplier * pivot for mine, pivot in zip(cols[q], cols[p])]
            rows[p] = rows[p] * reciprocal
        for i in range(g, groups):
            for p in inside:
                factor = cols[p][i - g]
                if i == g:
                    factor = jnp.where(index > p, factor, 0.0)
                work[i] = work[i] - factor * rows[p]
    return jnp.concatenate([w * lax.rsqrt(d) for w, d in zip(work, scale)])[:, RANK:]


def factor_kernel(own_terms, other_terms, inverse, own_ortho, other_ortho):
    stacked = sum(
        lax.dot_general(terms[...], terms[...], CONTRACT_LAST, preferred_element_type=F32)
        for terms in (own_terms, other_terms)
    )

    def part(left, right):
        return stacked[left * RANK : (left + 1) * RANK, right * RANK : (right + 1) * RANK]

    small = part(0, 2) + part(2, 0) + part(1, 1)
    gram = part(0, 0) + ((part(0, 1) + part(1, 0)) + small)
    lower_inverse = inverse_of_lower(gram)
    inverse[...] = lower_inverse
    for terms, ortho in ((own_terms, own_ortho), (other_terms, other_ortho)):
        for chunk in range(CHUNKS):
            cols = in_half(chunk)
            p_t = (
                terms[:RANK, cols].astype(F32)
                + terms[RANK : 2 * RANK, cols].astype(F32)
                + terms[2 * RANK :, cols].astype(F32)
            )
            ortho_t = jnp.dot(
                lower_inverse, p_t, precision=lax.Precision.HIGHEST, preferred_element_type=F32
            )
            high, low = two_terms(ortho_t)
            ortho[:RANK, cols] = high
            ortho[RANK : 2 * RANK, cols] = low
            ortho[2 * RANK :, cols] = high


def factor(own_terms, other_terms):
    ortho = pltpu.VMEM((3 * RANK, HALF), BF16)
    return pl.pallas_call(
        factor_kernel,
        out_shape=(pltpu.VMEM((RANK, RANK), F32), ortho, ortho),
        in_specs=[VMEM] * 2,
        out_specs=[VMEM] * 3,
        compiler_params=params(12),
        cost_estimate=pl.CostEstimate(flops=10**9, bytes_accessed=10**7, transcendentals=0),
        name="factor",
    )(own_terms, other_terms)


def apply_kernel(
    own_comp,
    other_comp,
    own,
    across,
    left,
    right,
    inverse,
    own_ortho,
    other_ortho,
    new_errors,
    update,
    new_q,
    error_buf,
    update_buf,
    q_buf,
    error_sems,
    update_sems,
    q_sem,
):
    total = (own[...] + across[...]) + (left[...] + right[...])
    q_t = jnp.dot(
        inverse[...], total * (1.0 / X), precision=lax.Precision.HIGHEST, preferred_element_type=F32
    )
    q_buf[...] = q_t[:, :ROWS]
    copies = [pltpu.make_async_copy(q_buf, new_q, q_sem)]
    copies[0].start()
    high = q_t.astype(BF16).astype(F32)
    stacked = jnp.concatenate([high, high, q_t - high]).T[:ROWS].astype(BF16)
    for half, (comp, ortho) in enumerate(((own_comp, own_ortho), (other_comp, other_ortho))):
        start = half_start(half == 0)
        for chunk in range(CHUNKS):
            cols, at = in_half(chunk), in_hbm(start, chunk)
            approx = jnp.dot(stacked, ortho[:, cols], preferred_element_type=F32)
            error_buf[half, :, cols] = comp[:, cols] - approx
            update_buf[half, :, cols] = approx.astype(BF16)
            pair = [
                pltpu.make_async_copy(
                    error_buf.at[half, :, cols], new_errors.at[:, at], error_sems.at[half, chunk]
                ),
                pltpu.make_async_copy(
                    update_buf.at[half, :, cols], update.at[:, at], update_sems.at[half, chunk]
                ),
            ]
            for copy in pair:
                copy.start()
            copies += pair
    for copy in copies:
        copy.wait()


def apply(own_comp, other_comp, own, across, left, right, inverse, own_ortho, other_ortho):
    comps = [pltpu.with_memory_space_constraint(a, pltpu.VMEM) for a in (own_comp, other_comp)]
    return pl.pallas_call(
        apply_kernel,
        out_shape=(
            jax.ShapeDtypeStruct((ROWS, FEATURES), F32),
            jax.ShapeDtypeStruct((ROWS, FEATURES), BF16),
            jax.ShapeDtypeStruct((RANK, ROWS), F32),
        ),
        in_specs=[VMEM] * 9,
        out_specs=[HBM] * 3,
        scratch_shapes=[
            pltpu.VMEM((C, ROWS, HALF), F32),
            pltpu.VMEM((C, ROWS, HALF), BF16),
            pltpu.VMEM((RANK, ROWS), F32),
            pltpu.SemaphoreType.DMA((C, CHUNKS)),
            pltpu.SemaphoreType.DMA((C, CHUNKS)),
            pltpu.SemaphoreType.DMA,
        ],
        compiler_params=params(20),
        name="apply",
    )(*comps, own, across, left, right, inverse, own_ortho, other_ortho)


def shift(array, axis, size, step):
    return lax.ppermute(array, axis, [(i, (i + step) % size) for i in range(size)])


def add_up(blocks):
    terms = [blocks[i] for i in range(blocks.shape[0])]
    while len(terms) > 1:
        terms = [left + right for left, right in zip(terms[::2], terms[1::2])]
    return terms[0]


def repeat(block, times):
    return jnp.broadcast_to(block, (times,) + block.shape)


def reduce_and_gather(mine):
    block = add_up(lax.all_to_all(mine, ("x", "y"), 0, 0))
    block = add_up(lax.all_to_all(repeat(block, Z), "z", 0, 0))
    return lax.all_to_all(repeat(block, BLOCKS), ("x", "y"), 0, 0)


def shards(grads, errors, q_start):
    q_t = q_start.T
    other_comp, other_low, other = compensate(grads[0], errors[0], q_t, False)
    received = shift(other, "c", C, 1)
    own_comp, own_low, mine = compensate(grads[0], errors[0], q_t, True)
    mine = reduce_and_gather(mine + received)
    other = shift(mine, "c", C, 1)
    product, own_terms = project(own_low, mine)
    product, other_terms = project(other_low, other, product)
    across, left, right = (shift(product, "x", X, step) for step in (2, 1, 3))
    inverse, own_ortho, other_ortho = factor(own_terms, other_terms)
    new_errors, update, new_q = apply(
        own_comp, other_comp, product, across, left, right, inverse, own_ortho, other_ortho
    )
    return (update, new_errors[None], new_q.T)


def solution(mesh):
    split = Mesh(mesh.devices.reshape(X, Y, Z, C), ("x", "y", "z", "c"))
    rows = ("y", "z", "c")
    return jax.shard_map(
        shards,
        mesh=split,
        in_specs=(P("x", rows, None), P("x", rows, None), P(rows, None)),
        out_specs=(P(rows, None), P("x", rows, None), P(rows, None)),
        check_vma=False,
    )
```

```python
import functools

import jax
import jax.numpy as jnp
from jax import lax
from jax.experimental import pallas as pl
from jax.experimental.pallas import tpu as pltpu
from jax.sharding import Mesh
from jax.sharding import PartitionSpec as P

X, Y, Z, C = 4, 4, 8, 2
RANK = 32
ROWS = 224
PAD = 256
FEATURES = 4096
HALF = FEATURES // C
BLOCKS = X * Y
BLOCK = HALF // BLOCKS
CHUNKS = 2
WIDTH = HALF // CHUNKS
GROUP = 8
F32, BF16 = jnp.float32, jnp.bfloat16
CONTRACT_LAST = (((1,), (1,)), ((), ()))
VMEM = pl.BlockSpec(memory_space=pltpu.VMEM)
HBM = pl.BlockSpec(memory_space=pltpu.HBM)


def half_start(own):
    core = lax.axis_index("c")
    return (core if own else 1 - core) * HALF


def in_hbm(start, chunk):
    return pl.ds(pl.multiple_of(start + chunk * WIDTH, WIDTH), WIDTH)


def in_half(chunk):
    return slice(chunk * WIDTH, (chunk + 1) * WIDTH)


def params(mebibytes):
    return pltpu.CompilerParams(vmem_limit_bytes=mebibytes * 2**20)


def two_terms(value):
    high = value.astype(BF16)
    return high, (value - high.astype(F32)).astype(BF16)


def three_terms(value):
    high = value.astype(BF16)
    rest = value - high.astype(F32)
    middle = rest.astype(BF16)
    return high, middle, (rest - middle.astype(F32)).astype(BF16)


def compensate_kernel(
    own, grads, errors, q_hbm, comp, low, partial, grad_buf, q_t, q_sem, grad_sems, error_sems
):
    start = half_start(own)
    q_copy = pltpu.make_async_copy(q_hbm, q_t, q_sem)
    q_copy.start()
    copies = []
    for chunk in range(CHUNKS):
        at, cols = in_hbm(start, chunk), in_half(chunk)
        pair = (
            pltpu.make_async_copy(grads.at[:, at], grad_buf.at[:, cols], grad_sems.at[chunk]),
            pltpu.make_async_copy(errors.at[:, at], comp.at[:, cols], error_sems.at[chunk]),
        )
        for copy in pair:
            copy.start()
        copies.append(pair)
    q_copy.wait()
    factor = q_t[...]
    for chunk in range(CHUNKS):
        for copy in copies[chunk]:
            copy.wait()
        cols = in_half(chunk)
        total = grad_buf[:, cols].astype(F32) + comp[:, cols]
        comp[:, cols] = total
        rounded = total.astype(BF16)
        low[:, cols] = rounded
        product = jnp.dot(factor, rounded, preferred_element_type=F32)
        for part in range(WIDTH // BLOCK):
            partial[chunk * (WIDTH // BLOCK) + part] = product[:, part * BLOCK : (part + 1) * BLOCK]


def compensate(grads, errors, q_t, own):
    operands = [pltpu.with_memory_space_constraint(a, pltpu.HBM) for a in (grads, errors, q_t)]
    return pl.pallas_call(
        functools.partial(compensate_kernel, own),
        out_shape=(
            pltpu.VMEM((ROWS, HALF), F32),
            pltpu.VMEM((ROWS, HALF), BF16),
            pltpu.VMEM((BLOCKS, RANK, BLOCK), F32),
        ),
        in_specs=[HBM] * 3,
        out_specs=[VMEM] * 3,
        scratch_shapes=[
            pltpu.VMEM((ROWS, HALF), BF16),
            pltpu.VMEM((RANK, ROWS), BF16),
            pltpu.SemaphoreType.DMA,
            pltpu.SemaphoreType.DMA((CHUNKS,)),
            pltpu.SemaphoreType.DMA((CHUNKS,)),
        ],
        compiler_params=params(12),
        cost_estimate=pl.CostEstimate(
            flops=2 * ROWS * HALF * RANK, bytes_accessed=6 * ROWS * HALF, transcendentals=0
        ),
        name="compensate_own" if own else "compensate_other",
    )(*operands)


def project_kernel(low, blocks, *refs):
    product, terms = refs[-2:]
    for block in range(BLOCKS):
        cols = slice(block * BLOCK, (block + 1) * BLOCK)
        for term, value in enumerate(three_terms(blocks[block])):
            terms[term * RANK : (term + 1) * RANK, cols] = value
    stacked = lax.dot_general(terms[...], low[...], CONTRACT_LAST, preferred_element_type=F32)
    total = stacked[:RANK] + (stacked[RANK : 2 * RANK] + stacked[2 * RANK :])
    if len(refs) == 3:
        total = total + refs[0][:, :ROWS]
    product[...] = jnp.zeros(product.shape, F32)
    product[:, :ROWS] = total


def project(low, blocks, *before):
    return pl.pallas_call(
        project_kernel,
        out_shape=(pltpu.VMEM((RANK, PAD), F32), pltpu.VMEM((3 * RANK, HALF), BF16)),
        in_specs=[VMEM] * (2 + len(before)),
        out_specs=[VMEM] * 2,
        compiler_params=params(12),
        cost_estimate=pl.CostEstimate(
            flops=6 * ROWS * HALF * RANK, bytes_accessed=2 * ROWS * HALF, transcendentals=0
        ),
        name="project",
    )(pltpu.with_memory_space_constraint(low, pltpu.VMEM), blocks, *before)


def inverse_of_lower(gram):
    shape = (GROUP, 2 * RANK)
    groups = RANK // GROUP
    row = lax.broadcasted_iota(jnp.int32, (RANK, RANK), 0)
    column = lax.broadcasted_iota(jnp.int32, (RANK, RANK), 1)
    whole = jnp.concatenate([gram, (row == column).astype(F32)], axis=1)
    work = [whole[g * GROUP : (g + 1) * GROUP] for g in range(groups)]
    index = lax.broadcasted_iota(jnp.int32, shape, 0)
    scale = [jnp.zeros(shape, F32) for _ in range(groups)]
    inside = range(GROUP)
    for g in range(groups):
        rows = [jnp.broadcast_to(work[g][p : p + 1, :], shape) for p in inside]
        cols = [
            [jnp.broadcast_to(work[i][:, g * GROUP + p : g * GROUP + p + 1], shape) for i in range(g, groups)]
            for p in inside
        ]
        entry = {
            (q, p): jnp.broadcast_to(cols[p][0][q : q + 1, :], shape) for p in inside for q in range(p, GROUP)
        }
        for p in inside:
            reciprocal = 1.0 / entry[p, p]
            scale[g] = jnp.where(index == p, entry[p, p], scale[g])
            for q in range(p + 1, GROUP):
                multiplier = entry[q, p] * reciprocal
                for t in range(q, GROUP):
                    entry[t, q] = entry[t, q] - multiplier * entry[t, p]
                rows[q] = rows[q] - multiplier * rows[p]
                cols[q] = [mine - multiplier * pivot for mine, pivot in zip(cols[q], cols[p])]
            rows[p] = rows[p] * reciprocal
        for i in range(g, groups):
            for p in inside:
                factor = cols[p][i - g]
                if i == g:
                    factor = jnp.where(index > p, factor, 0.0)
                work[i] = work[i] - factor * rows[p]
    return jnp.concatenate([w * lax.rsqrt(d) for w, d in zip(work, scale)])[:, RANK:]


def factor_kernel(own_terms, other_terms, inverse, own_ortho, other_ortho):
    stacked = sum(
        lax.dot_general(terms[...], terms[...], CONTRACT_LAST, preferred_element_type=F32)
        for terms in (own_terms, other_terms)
    )

    def part(left, right):
        return stacked[left * RANK : (left + 1) * RANK, right * RANK : (right + 1) * RANK]

    small = part(0, 2) + part(2, 0) + part(1, 1)
    gram = part(0, 0) + ((part(0, 1) + part(1, 0)) + small)
    lower_inverse = inverse_of_lower(gram)
    inverse[...] = lower_inverse
    one, two, three = (term.astype(F32) for term in three_terms(lower_inverse))
    weights = jnp.concatenate([one, one, two, one, two, three], axis=1).astype(BF16)
    for terms, ortho in ((own_terms, own_ortho), (other_terms, other_ortho)):
        for chunk in range(CHUNKS):
            cols = in_half(chunk)
            one, two, three = (terms[t * RANK : (t + 1) * RANK, cols] for t in range(3))
            stack = jnp.concatenate([one, two, one, three, two, one])
            high, low = two_terms(jnp.dot(weights, stack, preferred_element_type=F32))
            ortho[:RANK, cols] = high
            ortho[RANK:, cols] = low


def factor(own_terms, other_terms):
    ortho = pltpu.VMEM((2 * RANK, HALF), BF16)
    return pl.pallas_call(
        factor_kernel,
        out_shape=(pltpu.VMEM((RANK, RANK), F32), ortho, ortho),
        in_specs=[VMEM] * 2,
        out_specs=[VMEM] * 3,
        compiler_params=params(12),
        cost_estimate=pl.CostEstimate(flops=10**9, bytes_accessed=10**7, transcendentals=0),
        name="factor",
    )(own_terms, other_terms)


def apply_kernel(
    own_comp,
    other_comp,
    own,
    across,
    left,
    right,
    inverse,
    own_ortho,
    other_ortho,
    new_errors,
    update,
    new_q,
    error_buf,
    update_buf,
    q_buf,
    error_sems,
    update_sems,
    q_sem,
):
    total = (own[...] + across[...]) + (left[...] + right[...])
    q_t = jnp.dot(
        inverse[...], total * (1.0 / X), precision=lax.Precision.HIGHEST, preferred_element_type=F32
    )
    q_buf[...] = q_t[:, :ROWS]
    copies = [pltpu.make_async_copy(q_buf, new_q, q_sem)]
    copies[0].start()
    high = q_t.astype(BF16).astype(F32)
    stacked = jnp.concatenate([high, high, q_t - high]).T[:ROWS].astype(BF16)
    for half, (comp, ortho) in enumerate(((own_comp, own_ortho), (other_comp, other_ortho))):
        start = half_start(half == 0)
        for chunk in range(CHUNKS):
            cols, at = in_half(chunk), in_hbm(start, chunk)
            terms = ortho[:, cols]
            terms = jnp.concatenate([terms, terms[:RANK]])
            approx = jnp.dot(stacked, terms, preferred_element_type=F32)
            error_buf[half, :, cols] = comp[:, cols] - approx
            update_buf[half, :, cols] = approx.astype(BF16)
            pair = [
                pltpu.make_async_copy(
                    error_buf.at[half, :, cols], new_errors.at[:, at], error_sems.at[half, chunk]
                ),
                pltpu.make_async_copy(
                    update_buf.at[half, :, cols], update.at[:, at], update_sems.at[half, chunk]
                ),
            ]
            for copy in pair:
                copy.start()
            copies += pair
    for copy in copies:
        copy.wait()


def apply(own_comp, other_comp, own, across, left, right, inverse, own_ortho, other_ortho):
    comps = [pltpu.with_memory_space_constraint(a, pltpu.VMEM) for a in (own_comp, other_comp)]
    return pl.pallas_call(
        apply_kernel,
        out_shape=(
            jax.ShapeDtypeStruct((ROWS, FEATURES), F32),
            jax.ShapeDtypeStruct((ROWS, FEATURES), BF16),
            jax.ShapeDtypeStruct((RANK, ROWS), F32),
        ),
        in_specs=[VMEM] * 9,
        out_specs=[HBM] * 3,
        scratch_shapes=[
            pltpu.VMEM((C, ROWS, HALF), F32),
            pltpu.VMEM((C, ROWS, HALF), BF16),
            pltpu.VMEM((RANK, ROWS), F32),
            pltpu.SemaphoreType.DMA((C, CHUNKS)),
            pltpu.SemaphoreType.DMA((C, CHUNKS)),
            pltpu.SemaphoreType.DMA,
        ],
        compiler_params=params(20),
        name="apply",
    )(*comps, own, across, left, right, inverse, own_ortho, other_ortho)


def shift(array, axis, size, step):
    return lax.ppermute(array, axis, [(i, (i + step) % size) for i in range(size)])


def add_up(blocks):
    terms = [blocks[i] for i in range(blocks.shape[0])]
    while len(terms) > 1:
        terms = [left + right for left, right in zip(terms[::2], terms[1::2])]
    return terms[0]


def repeat(block, times):
    return jnp.broadcast_to(block, (times,) + block.shape)


def reduce_and_gather(mine):
    block = add_up(lax.all_to_all(mine, ("x", "y"), 0, 0))
    block = add_up(lax.all_to_all(repeat(block, Z), "z", 0, 0))
    return lax.all_to_all(repeat(block, BLOCKS), ("x", "y"), 0, 0)


def shards(grads, errors, q_start):
    q_t = q_start.T
    other_comp, other_low, other = compensate(grads[0], errors[0], q_t, False)
    received = shift(other, "c", C, 1)
    own_comp, own_low, mine = compensate(grads[0], errors[0], q_t, True)
    mine = reduce_and_gather(mine + received)
    other = shift(mine, "c", C, 1)
    product, own_terms = project(own_low, mine)
    product, other_terms = project(other_low, other, product)
    across, left, right = (shift(product, "x", X, step) for step in (2, 1, 3))
    inverse, own_ortho, other_ortho = factor(own_terms, other_terms)
    new_errors, update, new_q = apply(
        own_comp, other_comp, product, across, left, right, inverse, own_ortho, other_ortho
    )
    return (update, new_errors[None], new_q.T)


def solution(mesh):
    split = Mesh(mesh.devices.reshape(X, Y, Z, C), ("x", "y", "z", "c"))
    rows = ("y", "z", "c")
    return jax.shard_map(
        shards,
        mesh=split,
        in_specs=(P("x", rows, None), P("x", rows, None), P(rows, None)),
        out_specs=(P(rows, None), P("x", rows, None), P(rows, None)),
        check_vma=False,
    )
```

```python
import functools

import jax
import jax.numpy as jnp
from jax import lax
from jax.experimental import pallas as pl
from jax.experimental.pallas import tpu as pltpu
from jax.sharding import Mesh
from jax.sharding import PartitionSpec as P

X, Y, Z, C = 4, 4, 8, 2
RANK = 32
ROWS = 224
PAD = 256
FEATURES = 4096
HALF = FEATURES // C
BLOCKS = X * Y
BLOCK = HALF // BLOCKS
CHUNKS = 2
WIDTH = HALF // CHUNKS
GROUP = 8
SWAP = (1, 0)
REPLICAS = ((1, 0, 3, 2), (3, 2, 0, 1), (2, 3, 1, 0))
F32, BF16 = jnp.float32, jnp.bfloat16
CONTRACT_LAST = (((1,), (1,)), ((), ()))
VMEM = pl.BlockSpec(memory_space=pltpu.VMEM)
HBM = pl.BlockSpec(memory_space=pltpu.HBM)


def half_start(own):
    core = lax.axis_index("c")
    return (core if own else 1 - core) * HALF


def in_hbm(start, chunk):
    return pl.ds(pl.multiple_of(start + chunk * WIDTH, WIDTH), WIDTH)


def in_half(chunk):
    return slice(chunk * WIDTH, (chunk + 1) * WIDTH)


def params(mebibytes):
    return pltpu.CompilerParams(vmem_limit_bytes=mebibytes * 2**20)


def two_terms(value):
    high = value.astype(BF16)
    return high, (value - high.astype(F32)).astype(BF16)


def three_terms(value):
    high = value.astype(BF16)
    rest = value - high.astype(F32)
    middle = rest.astype(BF16)
    return high, middle, (rest - middle.astype(F32)).astype(BF16)


def compensate_kernel(
    own, grads, errors, q_hbm, comp, low, partial, grad_buf, q_t, q_sem, grad_sems, error_sems
):
    start = half_start(own)
    q_copy = pltpu.make_async_copy(q_hbm, q_t, q_sem)
    q_copy.start()
    copies = []
    for chunk in range(CHUNKS):
        at, cols = in_hbm(start, chunk), in_half(chunk)
        pair = (
            pltpu.make_async_copy(grads.at[:, at], grad_buf.at[:, cols], grad_sems.at[chunk]),
            pltpu.make_async_copy(errors.at[:, at], comp.at[:, cols], error_sems.at[chunk]),
        )
        for copy in pair:
            copy.start()
        copies.append(pair)
    q_copy.wait()
    factor = q_t[...]
    for chunk in range(CHUNKS):
        for copy in copies[chunk]:
            copy.wait()
        cols = in_half(chunk)
        total = grad_buf[:, cols].astype(F32) + comp[:, cols]
        comp[:, cols] = total
        rounded = total.astype(BF16)
        low[:, cols] = rounded
        product = jnp.dot(factor, rounded, preferred_element_type=F32)
        for part in range(WIDTH // BLOCK):
            partial[chunk * (WIDTH // BLOCK) + part] = product[:, part * BLOCK : (part + 1) * BLOCK]


def compensate(grads, errors, q_t, own):
    operands = [pltpu.with_memory_space_constraint(a, pltpu.HBM) for a in (grads, errors, q_t)]
    return pl.pallas_call(
        functools.partial(compensate_kernel, own),
        out_shape=(
            pltpu.VMEM((ROWS, HALF), F32),
            pltpu.VMEM((ROWS, HALF), BF16),
            pltpu.VMEM((BLOCKS, RANK, BLOCK), F32),
        ),
        in_specs=[HBM] * 3,
        out_specs=[VMEM] * 3,
        scratch_shapes=[
            pltpu.VMEM((ROWS, HALF), BF16),
            pltpu.VMEM((RANK, ROWS), BF16),
            pltpu.SemaphoreType.DMA,
            pltpu.SemaphoreType.DMA((CHUNKS,)),
            pltpu.SemaphoreType.DMA((CHUNKS,)),
        ],
        compiler_params=params(12),
        cost_estimate=pl.CostEstimate(
            flops=2 * ROWS * HALF * RANK, bytes_accessed=6 * ROWS * HALF, transcendentals=0
        ),
        name="compensate_own" if own else "compensate_other",
    )(*operands)


def project_kernel(low, blocks, *refs):
    product, terms = refs[-2:]
    for block in range(BLOCKS):
        cols = slice(block * BLOCK, (block + 1) * BLOCK)
        for term, value in enumerate(three_terms(blocks[block])):
            terms[term * RANK : (term + 1) * RANK, cols] = value
    stacked = lax.dot_general(terms[...], low[...], CONTRACT_LAST, preferred_element_type=F32)
    total = stacked[:RANK] + (stacked[RANK : 2 * RANK] + stacked[2 * RANK :])
    if len(refs) == 3:
        total = total + refs[0][:, :ROWS]
    product[...] = jnp.zeros(product.shape, F32)
    product[:, :ROWS] = total


def project(low, blocks, *before):
    return pl.pallas_call(
        project_kernel,
        out_shape=(pltpu.VMEM((RANK, PAD), F32), pltpu.VMEM((3 * RANK, HALF), BF16)),
        in_specs=[VMEM] * (2 + len(before)),
        out_specs=[VMEM] * 2,
        compiler_params=params(12),
        cost_estimate=pl.CostEstimate(
            flops=6 * ROWS * HALF * RANK, bytes_accessed=2 * ROWS * HALF, transcendentals=0
        ),
        name="project",
    )(pltpu.with_memory_space_constraint(low, pltpu.VMEM), blocks, *before)


def inverse_of_lower(gram):
    shape = (GROUP, 2 * RANK)
    groups = RANK // GROUP
    row = lax.broadcasted_iota(jnp.int32, (RANK, RANK), 0)
    column = lax.broadcasted_iota(jnp.int32, (RANK, RANK), 1)
    whole = jnp.concatenate([gram, (row == column).astype(F32)], axis=1)
    work = [whole[g * GROUP : (g + 1) * GROUP] for g in range(groups)]
    index = lax.broadcasted_iota(jnp.int32, shape, 0)
    scale = [jnp.zeros(shape, F32) for _ in range(groups)]
    inside = range(GROUP)
    for g in range(groups):
        rows = [jnp.broadcast_to(work[g][p : p + 1, :], shape) for p in inside]
        cols = [
            [jnp.broadcast_to(work[i][:, g * GROUP + p : g * GROUP + p + 1], shape) for i in range(g, groups)]
            for p in inside
        ]
        entry = {
            (q, p): jnp.broadcast_to(cols[p][0][q : q + 1, :], shape) for p in inside for q in range(p, GROUP)
        }
        for p in inside:
            reciprocal = 1.0 / entry[p, p]
            scale[g] = jnp.where(index == p, entry[p, p], scale[g])
            for q in range(p + 1, GROUP):
                multiplier = entry[q, p] * reciprocal
                for t in range(q, GROUP):
                    entry[t, q] = entry[t, q] - multiplier * entry[t, p]
                rows[q] = rows[q] - multiplier * rows[p]
                cols[q] = [mine - multiplier * pivot for mine, pivot in zip(cols[q], cols[p])]
            rows[p] = rows[p] * reciprocal
        for i in range(g, groups):
            for p in inside:
                factor = cols[p][i - g]
                if i == g:
                    factor = jnp.where(index > p, factor, 0.0)
                work[i] = work[i] - factor * rows[p]
    return jnp.concatenate([w * lax.rsqrt(d) for w, d in zip(work, scale)])[:, RANK:]


def factor_kernel(own_terms, other_terms, inverse, own_ortho, other_ortho):
    stacked = sum(
        lax.dot_general(terms[...], terms[...], CONTRACT_LAST, preferred_element_type=F32)
        for terms in (own_terms, other_terms)
    )

    def part(left, right):
        return stacked[left * RANK : (left + 1) * RANK, right * RANK : (right + 1) * RANK]

    small = part(0, 2) + part(2, 0) + part(1, 1)
    gram = part(0, 0) + ((part(0, 1) + part(1, 0)) + small)
    lower_inverse = inverse_of_lower(gram)
    inverse[...] = lower_inverse
    one, two, three = (term.astype(F32) for term in three_terms(lower_inverse))
    weights = jnp.concatenate([one, one, two, one, two, three], axis=1).astype(BF16)
    for terms, ortho in ((own_terms, own_ortho), (other_terms, other_ortho)):
        for chunk in range(CHUNKS):
            cols = in_half(chunk)
            one, two, three = (terms[t * RANK : (t + 1) * RANK, cols] for t in range(3))
            stack = jnp.concatenate([one, two, one, three, two, one])
            high, low = two_terms(jnp.dot(weights, stack, preferred_element_type=F32))
            ortho[:RANK, cols] = high
            ortho[RANK:, cols] = low


def factor(own_terms, other_terms):
    ortho = pltpu.VMEM((2 * RANK, HALF), BF16)
    return pl.pallas_call(
        factor_kernel,
        out_shape=(pltpu.VMEM((RANK, RANK), F32), ortho, ortho),
        in_specs=[VMEM] * 2,
        out_specs=[VMEM] * 3,
        compiler_params=params(12),
        cost_estimate=pl.CostEstimate(flops=10**9, bytes_accessed=10**7, transcendentals=0),
        name="factor",
    )(own_terms, other_terms)


def apply_kernel(
    own_comp,
    other_comp,
    own,
    pair,
    first,
    second,
    inverse,
    own_ortho,
    other_ortho,
    new_errors,
    update,
    new_q,
    error_buf,
    update_buf,
    q_buf,
    error_sems,
    update_sems,
    q_sem,
):
    total = (own[...] + pair[...]) + (first[...] + second[...])
    q_t = jnp.dot(
        inverse[...], total * (1.0 / X), precision=lax.Precision.HIGHEST, preferred_element_type=F32
    )
    q_buf[...] = q_t[:, :ROWS]
    copies = [pltpu.make_async_copy(q_buf, new_q, q_sem)]
    copies[0].start()
    high = q_t.astype(BF16).astype(F32)
    stacked = jnp.concatenate([high, high, q_t - high]).T[:ROWS].astype(BF16)
    for half, (comp, ortho) in enumerate(((own_comp, own_ortho), (other_comp, other_ortho))):
        start = half_start(half == 0)
        for chunk in range(CHUNKS):
            cols, at = in_half(chunk), in_hbm(start, chunk)
            terms = ortho[:, cols]
            terms = jnp.concatenate([terms, terms[:RANK]])
            approx = jnp.dot(stacked, terms, preferred_element_type=F32)
            error_buf[half, :, cols] = comp[:, cols] - approx
            update_buf[half, :, cols] = approx.astype(BF16)
            outgoing = [
                pltpu.make_async_copy(
                    error_buf.at[half, :, cols], new_errors.at[:, at], error_sems.at[half, chunk]
                ),
                pltpu.make_async_copy(
                    update_buf.at[half, :, cols], update.at[:, at], update_sems.at[half, chunk]
                ),
            ]
            for copy in outgoing:
                copy.start()
            copies += outgoing
    for copy in copies:
        copy.wait()


def apply(own_comp, other_comp, own, pair, first, second, inverse, own_ortho, other_ortho):
    comps = [pltpu.with_memory_space_constraint(a, pltpu.VMEM) for a in (own_comp, other_comp)]
    return pl.pallas_call(
        apply_kernel,
        out_shape=(
            jax.ShapeDtypeStruct((ROWS, FEATURES), F32),
            jax.ShapeDtypeStruct((ROWS, FEATURES), BF16),
            jax.ShapeDtypeStruct((RANK, ROWS), F32),
        ),
        in_specs=[VMEM] * 9,
        out_specs=[HBM] * 3,
        scratch_shapes=[
            pltpu.VMEM((C, ROWS, HALF), F32),
            pltpu.VMEM((C, ROWS, HALF), BF16),
            pltpu.VMEM((RANK, ROWS), F32),
            pltpu.SemaphoreType.DMA((C, CHUNKS)),
            pltpu.SemaphoreType.DMA((C, CHUNKS)),
            pltpu.SemaphoreType.DMA,
        ],
        compiler_params=params(20),
        name="apply",
    )(*comps, own, pair, first, second, inverse, own_ortho, other_ortho)


def send(array, axis, targets):
    return lax.ppermute(array, axis, list(enumerate(targets)))


def add_up(blocks):
    terms = [blocks[i] for i in range(blocks.shape[0])]
    while len(terms) > 1:
        terms = [left + right for left, right in zip(terms[::2], terms[1::2])]
    return terms[0]


def repeat(block, times):
    return jnp.broadcast_to(block, (times,) + block.shape)


def reduce_and_gather(mine):
    block = add_up(lax.all_to_all(mine, ("x", "y"), 0, 0))
    block = add_up(lax.all_to_all(repeat(block, Z), "z", 0, 0))
    return lax.all_to_all(repeat(block, BLOCKS), ("x", "y"), 0, 0)


def shards(grads, errors, q_start):
    q_t = q_start.T
    other_comp, other_low, other = compensate(grads[0], errors[0], q_t, False)
    received = send(other, "c", SWAP)
    own_comp, own_low, mine = compensate(grads[0], errors[0], q_t, True)
    mine = reduce_and_gather(mine + received)
    other = send(mine, "c", SWAP)
    product, own_terms = project(own_low, mine)
    product, other_terms = project(other_low, other, product)
    pair, first, second = (send(product, "x", targets) for targets in REPLICAS)
    inverse, own_ortho, other_ortho = factor(own_terms, other_terms)
    new_errors, update, new_q = apply(
        own_comp, other_comp, product, pair, first, second, inverse, own_ortho, other_ortho
    )
    return (update, new_errors[None], new_q.T)


def solution(mesh):
    split = Mesh(mesh.devices.reshape(X, Y, Z, C), ("x", "y", "z", "c"))
    rows = ("y", "z", "c")
    return jax.shard_map(
        shards,
        mesh=split,
        in_specs=(P("x", rows, None), P("x", rows, None), P(rows, None)),
        out_specs=(P(rows, None), P("x", rows, None), P(rows, None)),
        check_vma=False,
    )
```

```python
import functools

import jax
import jax.numpy as jnp
from jax import lax
from jax.experimental import pallas as pl
from jax.experimental.pallas import tpu as pltpu
from jax.sharding import Mesh
from jax.sharding import PartitionSpec as P

X, Y, Z, C = 4, 4, 8, 2
RANK = 32
ROWS = 224
PAD = 256
FEATURES = 4096
HALF = FEATURES // C
BLOCKS = X * Y
BLOCK = HALF // BLOCKS
CHUNKS = 2
WIDTH = HALF // CHUNKS
GROUP = 8
SWAP = (1, 0)
REPLICAS = ((1, 0, 3, 2), (2, 3, 0, 1), (3, 2, 1, 0))
F32, BF16 = jnp.float32, jnp.bfloat16
CONTRACT_LAST = (((1,), (1,)), ((), ()))
VMEM = pl.BlockSpec(memory_space=pltpu.VMEM)
HBM = pl.BlockSpec(memory_space=pltpu.HBM)


def half_start(own):
    core = lax.axis_index("c")
    return (core if own else 1 - core) * HALF


def in_hbm(start, chunk):
    return pl.ds(pl.multiple_of(start + chunk * WIDTH, WIDTH), WIDTH)


def in_half(chunk):
    return slice(chunk * WIDTH, (chunk + 1) * WIDTH)


def params(mebibytes):
    return pltpu.CompilerParams(vmem_limit_bytes=mebibytes * 2**20)


def two_terms(value):
    high = value.astype(BF16)
    return high, (value - high.astype(F32)).astype(BF16)


def three_terms(value):
    high = value.astype(BF16)
    rest = value - high.astype(F32)
    middle = rest.astype(BF16)
    return high, middle, (rest - middle.astype(F32)).astype(BF16)


def compensate_kernel(
    own, grads, errors, q_hbm, comp, low, partial, grad_buf, q_t, q_sem, grad_sems, error_sems
):
    start = half_start(own)
    q_copy = pltpu.make_async_copy(q_hbm, q_t, q_sem)
    q_copy.start()
    copies = []
    for chunk in range(CHUNKS):
        at, cols = in_hbm(start, chunk), in_half(chunk)
        pair = (
            pltpu.make_async_copy(grads.at[:, at], grad_buf.at[:, cols], grad_sems.at[chunk]),
            pltpu.make_async_copy(errors.at[:, at], comp.at[:, cols], error_sems.at[chunk]),
        )
        for copy in pair:
            copy.start()
        copies.append(pair)
    q_copy.wait()
    factor = q_t[...]
    for chunk in range(CHUNKS):
        for copy in copies[chunk]:
            copy.wait()
        cols = in_half(chunk)
        total = grad_buf[:, cols].astype(F32) + comp[:, cols]
        comp[:, cols] = total
        rounded = total.astype(BF16)
        low[:, cols] = rounded
        product = jnp.dot(factor, rounded, preferred_element_type=F32)
        for part in range(WIDTH // BLOCK):
            partial[chunk * (WIDTH // BLOCK) + part] = product[:, part * BLOCK : (part + 1) * BLOCK]


def compensate(grads, errors, q_t, own):
    operands = [pltpu.with_memory_space_constraint(a, pltpu.HBM) for a in (grads, errors, q_t)]
    return pl.pallas_call(
        functools.partial(compensate_kernel, own),
        out_shape=(
            pltpu.VMEM((ROWS, HALF), F32),
            pltpu.VMEM((ROWS, HALF), BF16),
            pltpu.VMEM((BLOCKS, RANK, BLOCK), F32),
        ),
        in_specs=[HBM] * 3,
        out_specs=[VMEM] * 3,
        scratch_shapes=[
            pltpu.VMEM((ROWS, HALF), BF16),
            pltpu.VMEM((RANK, ROWS), BF16),
            pltpu.SemaphoreType.DMA,
            pltpu.SemaphoreType.DMA((CHUNKS,)),
            pltpu.SemaphoreType.DMA((CHUNKS,)),
        ],
        compiler_params=params(12),
        cost_estimate=pl.CostEstimate(
            flops=2 * ROWS * HALF * RANK, bytes_accessed=6 * ROWS * HALF, transcendentals=0
        ),
        name="compensate_own" if own else "compensate_other",
    )(*operands)


def project_kernel(low, blocks, *refs):
    product, terms = refs[-2:]
    for block in range(BLOCKS):
        cols = slice(block * BLOCK, (block + 1) * BLOCK)
        for term, value in enumerate(three_terms(blocks[block])):
            terms[term * RANK : (term + 1) * RANK, cols] = value
    stacked = lax.dot_general(terms[...], low[...], CONTRACT_LAST, preferred_element_type=F32)
    total = stacked[:RANK] + (stacked[RANK : 2 * RANK] + stacked[2 * RANK :])
    if len(refs) == 3:
        total = total + refs[0][:, :ROWS]
    product[...] = jnp.zeros(product.shape, F32)
    product[:, :ROWS] = total


def project(low, blocks, *before):
    return pl.pallas_call(
        project_kernel,
        out_shape=(pltpu.VMEM((RANK, PAD), F32), pltpu.VMEM((3 * RANK, HALF), BF16)),
        in_specs=[VMEM] * (2 + len(before)),
        out_specs=[VMEM] * 2,
        compiler_params=params(12),
        cost_estimate=pl.CostEstimate(
            flops=6 * ROWS * HALF * RANK, bytes_accessed=2 * ROWS * HALF, transcendentals=0
        ),
        name="project",
    )(pltpu.with_memory_space_constraint(low, pltpu.VMEM), blocks, *before)


def inverse_of_lower(gram):
    shape = (GROUP, 2 * RANK)
    groups = RANK // GROUP
    row = lax.broadcasted_iota(jnp.int32, (RANK, RANK), 0)
    column = lax.broadcasted_iota(jnp.int32, (RANK, RANK), 1)
    whole = jnp.concatenate([gram, (row == column).astype(F32)], axis=1)
    work = [whole[g * GROUP : (g + 1) * GROUP] for g in range(groups)]
    index = lax.broadcasted_iota(jnp.int32, shape, 0)
    scale = [jnp.zeros(shape, F32) for _ in range(groups)]
    inside = range(GROUP)
    for g in range(groups):
        rows = [jnp.broadcast_to(work[g][p : p + 1, :], shape) for p in inside]
        cols = [
            [jnp.broadcast_to(work[i][:, g * GROUP + p : g * GROUP + p + 1], shape) for i in range(g, groups)]
            for p in inside
        ]
        entry = {
            (q, p): jnp.broadcast_to(cols[p][0][q : q + 1, :], shape) for p in inside for q in range(p, GROUP)
        }
        for p in inside:
            reciprocal = 1.0 / entry[p, p]
            scale[g] = jnp.where(index == p, entry[p, p], scale[g])
            for q in range(p + 1, GROUP):
                multiplier = entry[q, p] * reciprocal
                for t in range(q, GROUP):
                    entry[t, q] = entry[t, q] - multiplier * entry[t, p]
                rows[q] = rows[q] - multiplier * rows[p]
                cols[q] = [mine - multiplier * pivot for mine, pivot in zip(cols[q], cols[p])]
            rows[p] = rows[p] * reciprocal
        for i in range(g, groups):
            for p in inside:
                factor = cols[p][i - g]
                if i == g:
                    factor = jnp.where(index > p, factor, 0.0)
                work[i] = work[i] - factor * rows[p]
    return jnp.concatenate([w * lax.rsqrt(d) for w, d in zip(work, scale)])[:, RANK:]


def factor_kernel(own_terms, other_terms, inverse, own_ortho, other_ortho):
    stacked = sum(
        lax.dot_general(terms[...], terms[...], CONTRACT_LAST, preferred_element_type=F32)
        for terms in (own_terms, other_terms)
    )

    def part(left, right):
        return stacked[left * RANK : (left + 1) * RANK, right * RANK : (right + 1) * RANK]

    small = part(0, 2) + part(2, 0) + part(1, 1)
    gram = part(0, 0) + ((part(0, 1) + part(1, 0)) + small)
    lower_inverse = inverse_of_lower(gram)
    inverse[...] = lower_inverse
    one, two, three = (term.astype(F32) for term in three_terms(lower_inverse))
    weights = jnp.concatenate([one, one, two, one, two, three], axis=1).astype(BF16)
    for terms, ortho in ((own_terms, own_ortho), (other_terms, other_ortho)):
        for chunk in range(CHUNKS):
            cols = in_half(chunk)
            one, two, three = (terms[t * RANK : (t + 1) * RANK, cols] for t in range(3))
            stack = jnp.concatenate([one, two, one, three, two, one])
            high, low = two_terms(jnp.dot(weights, stack, preferred_element_type=F32))
            ortho[:RANK, cols] = high
            ortho[RANK:, cols] = low


def factor(own_terms, other_terms):
    ortho = pltpu.VMEM((2 * RANK, HALF), BF16)
    return pl.pallas_call(
        factor_kernel,
        out_shape=(pltpu.VMEM((RANK, RANK), F32), ortho, ortho),
        in_specs=[VMEM] * 2,
        out_specs=[VMEM] * 3,
        compiler_params=params(12),
        cost_estimate=pl.CostEstimate(flops=10**9, bytes_accessed=10**7, transcendentals=0),
        name="factor",
    )(own_terms, other_terms)


def apply_kernel(
    own_comp,
    other_comp,
    own,
    pair,
    first,
    second,
    inverse,
    own_ortho,
    other_ortho,
    new_errors,
    update,
    new_q,
    error_buf,
    update_buf,
    q_buf,
    error_sems,
    update_sems,
    q_sem,
):
    total = (own[...] + pair[...]) + (first[...] + second[...])
    q_t = jnp.dot(
        inverse[...], total * (1.0 / X), precision=lax.Precision.HIGHEST, preferred_element_type=F32
    )
    q_buf[...] = q_t[:, :ROWS]
    copies = [pltpu.make_async_copy(q_buf, new_q, q_sem)]
    copies[0].start()
    high = q_t.astype(BF16).astype(F32)
    stacked = jnp.concatenate([high, high, q_t - high]).T[:ROWS].astype(BF16)
    for half, (comp, ortho) in enumerate(((own_comp, own_ortho), (other_comp, other_ortho))):
        start = half_start(half == 0)
        for chunk in range(CHUNKS):
            cols, at = in_half(chunk), in_hbm(start, chunk)
            terms = ortho[:, cols]
            terms = jnp.concatenate([terms, terms[:RANK]])
            approx = jnp.dot(stacked, terms, preferred_element_type=F32)
            update_buf[half, :, cols] = approx.astype(BF16)
            update_copy = pltpu.make_async_copy(
                update_buf.at[half, :, cols], update.at[:, at], update_sems.at[half, chunk]
            )
            update_copy.start()
            error_buf[half, :, cols] = comp[:, cols] - approx
            error_copy = pltpu.make_async_copy(
                error_buf.at[half, :, cols], new_errors.at[:, at], error_sems.at[half, chunk]
            )
            error_copy.start()
            copies += [update_copy, error_copy]
    for copy in copies:
        copy.wait()


def apply(own_comp, other_comp, own, pair, first, second, inverse, own_ortho, other_ortho):
    comps = [pltpu.with_memory_space_constraint(a, pltpu.VMEM) for a in (own_comp, other_comp)]
    return pl.pallas_call(
        apply_kernel,
        out_shape=(
            jax.ShapeDtypeStruct((ROWS, FEATURES), F32),
            jax.ShapeDtypeStruct((ROWS, FEATURES), BF16),
            jax.ShapeDtypeStruct((RANK, ROWS), F32),
        ),
        in_specs=[VMEM] * 9,
        out_specs=[HBM] * 3,
        scratch_shapes=[
            pltpu.VMEM((C, ROWS, HALF), F32),
            pltpu.VMEM((C, ROWS, HALF), BF16),
            pltpu.VMEM((RANK, ROWS), F32),
            pltpu.SemaphoreType.DMA((C, CHUNKS)),
            pltpu.SemaphoreType.DMA((C, CHUNKS)),
            pltpu.SemaphoreType.DMA,
        ],
        compiler_params=params(20),
        name="apply",
    )(*comps, own, pair, first, second, inverse, own_ortho, other_ortho)


def send(array, axis, targets):
    return lax.ppermute(array, axis, list(enumerate(targets)))


def add_up(blocks):
    terms = [blocks[i] for i in range(blocks.shape[0])]
    while len(terms) > 1:
        terms = [left + right for left, right in zip(terms[::2], terms[1::2])]
    return terms[0]


def repeat(block, times):
    return jnp.broadcast_to(block, (times,) + block.shape)


def reduce_and_gather(mine):
    block = add_up(lax.all_to_all(mine, ("x", "y"), 0, 0))
    block = add_up(lax.all_to_all(repeat(block, Z), "z", 0, 0))
    return lax.all_to_all(repeat(block, BLOCKS), ("x", "y"), 0, 0)


def shards(grads, errors, q_start):
    q_t = q_start.T
    other_comp, other_low, other = compensate(grads[0], errors[0], q_t, False)
    received = send(other, "c", SWAP)
    own_comp, own_low, mine = compensate(grads[0], errors[0], q_t, True)
    mine = reduce_and_gather(mine + received)
    other = send(mine, "c", SWAP)
    product, own_terms = project(own_low, mine)
    product, other_terms = project(other_low, other, product)
    pair, first, second = (send(product, "x", targets) for targets in REPLICAS)
    inverse, own_ortho, other_ortho = factor(own_terms, other_terms)
    new_errors, update, new_q = apply(
        own_comp, other_comp, product, pair, first, second, inverse, own_ortho, other_ortho
    )
    return (update, new_errors[None], new_q.T)


def solution(mesh):
    split = Mesh(mesh.devices.reshape(X, Y, Z, C), ("x", "y", "z", "c"))
    rows = ("y", "z", "c")
    return jax.shard_map(
        shards,
        mesh=split,
        in_specs=(P("x", rows, None), P("x", rows, None), P(rows, None)),
        out_specs=(P(rows, None), P("x", rows, None), P(rows, None)),
        check_vma=False,
    )
```

```python
import functools

import jax
import jax.numpy as jnp
from jax import lax
from jax.experimental import pallas as pl
from jax.experimental.pallas import tpu as pltpu
from jax.sharding import Mesh
from jax.sharding import PartitionSpec as P

X, Y, Z, C = 4, 4, 8, 2
RANK = 32
ROWS = 224
PAD = 256
FEATURES = 4096
HALF = FEATURES // C
BLOCKS = X * Y
BLOCK = HALF // BLOCKS
CHUNKS = 2
WIDTH = HALF // CHUNKS
GROUP = 8
SWAP = (1, 0)
REPLICAS = ((1, 0, 3, 2), (2, 3, 0, 1), (3, 2, 1, 0))
F32, BF16 = jnp.float32, jnp.bfloat16
CONTRACT_LAST = (((1,), (1,)), ((), ()))
VMEM = pl.BlockSpec(memory_space=pltpu.VMEM)
HBM = pl.BlockSpec(memory_space=pltpu.HBM)


def half_start(own):
    core = lax.axis_index("c")
    return (core if own else 1 - core) * HALF


def in_hbm(start, chunk):
    return pl.ds(pl.multiple_of(start + chunk * WIDTH, WIDTH), WIDTH)


def in_half(chunk):
    return slice(chunk * WIDTH, (chunk + 1) * WIDTH)


def params(mebibytes):
    return pltpu.CompilerParams(vmem_limit_bytes=mebibytes * 2**20)


def two_terms(value):
    high = value.astype(BF16)
    return high, (value - high.astype(F32)).astype(BF16)


def three_terms(value):
    high = value.astype(BF16)
    rest = value - high.astype(F32)
    middle = rest.astype(BF16)
    return high, middle, (rest - middle.astype(F32)).astype(BF16)


def compensate_kernel(
    own, grads, errors, q_hbm, comp, low, partial, grad_buf, q_t, q_sem, grad_sems, error_sems
):
    start = half_start(own)
    q_copy = pltpu.make_async_copy(q_hbm, q_t, q_sem)
    q_copy.start()
    copies = []
    for chunk in range(CHUNKS):
        at, cols = in_hbm(start, chunk), in_half(chunk)
        pair = (
            pltpu.make_async_copy(grads.at[:, at], grad_buf.at[:, cols], grad_sems.at[chunk]),
            pltpu.make_async_copy(errors.at[:, at], comp.at[:, cols], error_sems.at[chunk]),
        )
        for copy in pair:
            copy.start()
        copies.append(pair)
    q_copy.wait()
    factor = q_t[...]
    for chunk in range(CHUNKS):
        for copy in copies[chunk]:
            copy.wait()
        cols = in_half(chunk)
        total = grad_buf[:, cols].astype(F32) + comp[:, cols]
        comp[:, cols] = total
        rounded = total.astype(BF16)
        low[:, cols] = rounded
        product = jnp.dot(factor, rounded, preferred_element_type=F32)
        for part in range(WIDTH // BLOCK):
            partial[chunk * (WIDTH // BLOCK) + part] = product[:, part * BLOCK : (part + 1) * BLOCK]


def compensate(grads, errors, q_t, own):
    operands = [pltpu.with_memory_space_constraint(a, pltpu.HBM) for a in (grads, errors, q_t)]
    return pl.pallas_call(
        functools.partial(compensate_kernel, own),
        out_shape=(
            pltpu.VMEM((ROWS, HALF), F32),
            pltpu.VMEM((ROWS, HALF), BF16),
            pltpu.VMEM((BLOCKS, RANK, BLOCK), F32),
        ),
        in_specs=[HBM] * 3,
        out_specs=[VMEM] * 3,
        scratch_shapes=[
            pltpu.VMEM((ROWS, HALF), BF16),
            pltpu.VMEM((RANK, ROWS), BF16),
            pltpu.SemaphoreType.DMA,
            pltpu.SemaphoreType.DMA((CHUNKS,)),
            pltpu.SemaphoreType.DMA((CHUNKS,)),
        ],
        compiler_params=params(12),
        cost_estimate=pl.CostEstimate(
            flops=2 * ROWS * HALF * RANK, bytes_accessed=6 * ROWS * HALF, transcendentals=0
        ),
        name="compensate_own" if own else "compensate_other",
    )(*operands)


def project_kernel(low, blocks, *refs):
    product, terms = refs[-2:]
    for block in range(BLOCKS):
        cols = slice(block * BLOCK, (block + 1) * BLOCK)
        for term, value in enumerate(three_terms(blocks[block])):
            terms[term * RANK : (term + 1) * RANK, cols] = value
    stacked = lax.dot_general(terms[...], low[...], CONTRACT_LAST, preferred_element_type=F32)
    total = stacked[:RANK] + (stacked[RANK : 2 * RANK] + stacked[2 * RANK :])
    if len(refs) == 3:
        total = total + refs[0][:, :ROWS]
    product[...] = jnp.zeros(product.shape, F32)
    product[:, :ROWS] = total


def project(low, blocks, *before):
    return pl.pallas_call(
        project_kernel,
        out_shape=(pltpu.VMEM((RANK, PAD), F32), pltpu.VMEM((3 * RANK, HALF), BF16)),
        in_specs=[VMEM] * (2 + len(before)),
        out_specs=[VMEM] * 2,
        compiler_params=params(12),
        cost_estimate=pl.CostEstimate(
            flops=6 * ROWS * HALF * RANK, bytes_accessed=2 * ROWS * HALF, transcendentals=0
        ),
        name="project",
    )(pltpu.with_memory_space_constraint(low, pltpu.VMEM), blocks, *before)


def inverse_of_lower(gram):
    shape = (GROUP, 2 * RANK)
    groups = RANK // GROUP
    row = lax.broadcasted_iota(jnp.int32, (RANK, RANK), 0)
    column = lax.broadcasted_iota(jnp.int32, (RANK, RANK), 1)
    whole = jnp.concatenate([gram, (row == column).astype(F32)], axis=1)
    work = [whole[g * GROUP : (g + 1) * GROUP] for g in range(groups)]
    index = lax.broadcasted_iota(jnp.int32, shape, 0)
    scale = [jnp.zeros(shape, F32) for _ in range(groups)]
    inside = range(GROUP)
    for g in range(groups):
        rows = [jnp.broadcast_to(work[g][p : p + 1, :], shape) for p in inside]
        cols = [
            [jnp.broadcast_to(work[i][:, g * GROUP + p : g * GROUP + p + 1], shape) for i in range(g, groups)]
            for p in inside
        ]
        entry = {
            (q, p): jnp.broadcast_to(cols[p][0][q : q + 1, :], shape) for p in inside for q in range(p, GROUP)
        }
        for p in inside:
            reciprocal = 1.0 / entry[p, p]
            scale[g] = jnp.where(index == p, entry[p, p], scale[g])
            for q in range(p + 1, GROUP):
                multiplier = entry[q, p] * reciprocal
                for t in range(q, GROUP):
                    entry[t, q] = entry[t, q] - multiplier * entry[t, p]
                rows[q] = rows[q] - multiplier * rows[p]
                cols[q] = [mine - multiplier * pivot for mine, pivot in zip(cols[q], cols[p])]
            rows[p] = rows[p] * reciprocal
        for i in range(g, groups):
            for p in inside:
                factor = cols[p][i - g]
                if i == g:
                    factor = jnp.where(index > p, factor, 0.0)
                work[i] = work[i] - factor * rows[p]
    return jnp.concatenate([w * lax.rsqrt(d) for w, d in zip(work, scale)])[:, RANK:]


def ortho_terms(weights, terms):
    one, two, three = (terms[t * RANK : (t + 1) * RANK] for t in range(3))
    stack = jnp.concatenate([one, two, one, three, two, one])
    return jnp.concatenate(two_terms(jnp.dot(weights, stack, preferred_element_type=F32)))


def factor_kernel(own_terms, other_terms, inverse, weights, ortho):
    stacked = sum(
        lax.dot_general(terms[...], terms[...], CONTRACT_LAST, preferred_element_type=F32)
        for terms in (own_terms, other_terms)
    )

    def part(left, right):
        return stacked[left * RANK : (left + 1) * RANK, right * RANK : (right + 1) * RANK]

    small = part(0, 2) + part(2, 0) + part(1, 1)
    gram = part(0, 0) + ((part(0, 1) + part(1, 0)) + small)
    lower_inverse = inverse_of_lower(gram)
    inverse[...] = lower_inverse
    one, two, three = (term.astype(F32) for term in three_terms(lower_inverse))
    beside = jnp.concatenate([one, one, two, one, two, three], axis=1).astype(BF16)
    weights[...] = beside
    ortho[...] = ortho_terms(beside, own_terms[:, in_half(0)])


def factor(own_terms, other_terms):
    return pl.pallas_call(
        factor_kernel,
        out_shape=(
            pltpu.VMEM((RANK, RANK), F32),
            pltpu.VMEM((RANK, 6 * RANK), BF16),
            pltpu.VMEM((2 * RANK, WIDTH), BF16),
        ),
        in_specs=[VMEM] * 2,
        out_specs=[VMEM] * 3,
        compiler_params=params(12),
        cost_estimate=pl.CostEstimate(flops=10**9, bytes_accessed=10**7, transcendentals=0),
        name="factor",
    )(own_terms, other_terms)


def apply_kernel(
    own_comp,
    other_comp,
    own,
    pair,
    first,
    second,
    inverse,
    weights,
    first_ortho,
    own_terms,
    other_terms,
    new_errors,
    update,
    new_q,
    error_buf,
    update_buf,
    q_buf,
    error_sems,
    update_sems,
    q_sem,
):
    total = (own[...] + pair[...]) + (first[...] + second[...])
    q_t = jnp.dot(
        inverse[...], total * (1.0 / X), precision=lax.Precision.HIGHEST, preferred_element_type=F32
    )
    q_buf[...] = q_t[:, :ROWS]
    copies = [pltpu.make_async_copy(q_buf, new_q, q_sem)]
    copies[0].start()
    high = q_t.astype(BF16).astype(F32)
    stacked = jnp.concatenate([high, high, q_t - high]).T[:ROWS].astype(BF16)
    for half, (comp, terms) in enumerate(((own_comp, own_terms), (other_comp, other_terms))):
        start = half_start(half == 0)
        for chunk in range(CHUNKS):
            cols, at = in_half(chunk), in_hbm(start, chunk)
            ready = half == 0 and chunk == 0
            ortho = first_ortho[...] if ready else ortho_terms(weights[...], terms[:, cols])
            ortho = jnp.concatenate([ortho, ortho[:RANK]])
            approx = jnp.dot(stacked, ortho, preferred_element_type=F32)
            update_buf[half, :, cols] = approx.astype(BF16)
            update_copy = pltpu.make_async_copy(
                update_buf.at[half, :, cols], update.at[:, at], update_sems.at[half, chunk]
            )
            update_copy.start()
            error_buf[half, :, cols] = comp[:, cols] - approx
            error_copy = pltpu.make_async_copy(
                error_buf.at[half, :, cols], new_errors.at[:, at], error_sems.at[half, chunk]
            )
            error_copy.start()
            copies += [update_copy, error_copy]
    for copy in copies:
        copy.wait()


def apply(own_comp, other_comp, *operands):
    comps = [pltpu.with_memory_space_constraint(a, pltpu.VMEM) for a in (own_comp, other_comp)]
    return pl.pallas_call(
        apply_kernel,
        out_shape=(
            jax.ShapeDtypeStruct((ROWS, FEATURES), F32),
            jax.ShapeDtypeStruct((ROWS, FEATURES), BF16),
            jax.ShapeDtypeStruct((RANK, ROWS), F32),
        ),
        in_specs=[VMEM] * (2 + len(operands)),
        out_specs=[HBM] * 3,
        scratch_shapes=[
            pltpu.VMEM((C, ROWS, HALF), F32),
            pltpu.VMEM((C, ROWS, HALF), BF16),
            pltpu.VMEM((RANK, ROWS), F32),
            pltpu.SemaphoreType.DMA((C, CHUNKS)),
            pltpu.SemaphoreType.DMA((C, CHUNKS)),
            pltpu.SemaphoreType.DMA,
        ],
        compiler_params=params(20),
        name="apply",
    )(*comps, *operands)


def send(array, axis, targets):
    return lax.ppermute(array, axis, list(enumerate(targets)))


def add_up(blocks):
    terms = [blocks[i] for i in range(blocks.shape[0])]
    while len(terms) > 1:
        terms = [left + right for left, right in zip(terms[::2], terms[1::2])]
    return terms[0]


def repeat(block, times):
    return jnp.broadcast_to(block, (times,) + block.shape)


def reduce_and_gather(mine):
    block = add_up(lax.all_to_all(mine, ("x", "y"), 0, 0))
    block = add_up(lax.all_to_all(repeat(block, Z), "z", 0, 0))
    return lax.all_to_all(repeat(block, BLOCKS), ("x", "y"), 0, 0)


def shards(grads, errors, q_start):
    q_t = q_start.T
    other_comp, other_low, other = compensate(grads[0], errors[0], q_t, False)
    received = send(other, "c", SWAP)
    own_comp, own_low, mine = compensate(grads[0], errors[0], q_t, True)
    mine = reduce_and_gather(mine + received)
    other = send(mine, "c", SWAP)
    product, own_terms = project(own_low, mine)
    product, other_terms = project(other_low, other, product)
    pair, first, second = (send(product, "x", targets) for targets in REPLICAS)
    factors = factor(own_terms, other_terms)
    new_errors, update, new_q = apply(
        own_comp, other_comp, product, pair, first, second, *factors, own_terms, other_terms
    )
    return (update, new_errors[None], new_q.T)


def solution(mesh):
    split = Mesh(mesh.devices.reshape(X, Y, Z, C), ("x", "y", "z", "c"))
    rows = ("y", "z", "c")
    return jax.shard_map(
        shards,
        mesh=split,
        in_specs=(P("x", rows, None), P("x", rows, None), P(rows, None)),
        out_specs=(P(rows, None), P("x", rows, None), P(rows, None)),
        check_vma=False,
    )
```

```python
import functools

import jax
import jax.numpy as jnp
from jax import lax
from jax.experimental import pallas as pl
from jax.experimental.pallas import tpu as pltpu
from jax.sharding import Mesh
from jax.sharding import PartitionSpec as P

X, Y, Z, C = 4, 4, 8, 2
RANK = 32
ROWS = 224
PAD = 256
FEATURES = 4096
HALF = FEATURES // C
BLOCKS = X * Y
BLOCK = HALF // BLOCKS
CHUNKS = 2
WIDTH = HALF // CHUNKS
GROUP = 8
SWAP = (1, 0)
REPLICAS = ((1, 0, 3, 2), (2, 3, 0, 1), (3, 2, 1, 0))
OWNERS = [[C * z + (half + z // (Z // C)) % C for z in range(Z)] for half in range(C)]
F32, BF16 = jnp.float32, jnp.bfloat16
CONTRACT_LAST = (((1,), (1,)), ((), ()))
VMEM = pl.BlockSpec(memory_space=pltpu.VMEM)
HBM = pl.BlockSpec(memory_space=pltpu.HBM)


def half_start(own):
    half = lax.rem(lax.axis_index("c") + lax.div(lax.axis_index("z"), Z // C), C)
    return (half if own else 1 - half) * HALF


def in_hbm(start, chunk):
    return pl.ds(pl.multiple_of(start + chunk * WIDTH, WIDTH), WIDTH)


def in_half(chunk):
    return slice(chunk * WIDTH, (chunk + 1) * WIDTH)


def params(mebibytes):
    return pltpu.CompilerParams(vmem_limit_bytes=mebibytes * 2**20)


def two_terms(value):
    high = value.astype(BF16)
    return high, (value - high.astype(F32)).astype(BF16)


def three_terms(value):
    high = value.astype(BF16)
    rest = value - high.astype(F32)
    middle = rest.astype(BF16)
    return high, middle, (rest - middle.astype(F32)).astype(BF16)


def compensate_kernel(
    own, grads, errors, q_hbm, comp, low, partial, grad_buf, q_t, q_sem, grad_sems, error_sems
):
    start = half_start(own)
    q_copy = pltpu.make_async_copy(q_hbm, q_t, q_sem)
    q_copy.start()
    copies = []
    for chunk in range(CHUNKS):
        at, cols = in_hbm(start, chunk), in_half(chunk)
        pair = (
            pltpu.make_async_copy(grads.at[:, at], grad_buf.at[:, cols], grad_sems.at[chunk]),
            pltpu.make_async_copy(errors.at[:, at], comp.at[:, cols], error_sems.at[chunk]),
        )
        for copy in pair:
            copy.start()
        copies.append(pair)
    q_copy.wait()
    factor = q_t[...]
    for chunk in range(CHUNKS):
        for copy in copies[chunk]:
            copy.wait()
        cols = in_half(chunk)
        total = grad_buf[:, cols].astype(F32) + comp[:, cols]
        comp[:, cols] = total
        rounded = total.astype(BF16)
        low[:, cols] = rounded
        product = jnp.dot(factor, rounded, preferred_element_type=F32)
        for part in range(WIDTH // BLOCK):
            partial[chunk * (WIDTH // BLOCK) + part] = product[:, part * BLOCK : (part + 1) * BLOCK]


def compensate(grads, errors, q_t, own):
    operands = [pltpu.with_memory_space_constraint(a, pltpu.HBM) for a in (grads, errors, q_t)]
    return pl.pallas_call(
        functools.partial(compensate_kernel, own),
        out_shape=(
            pltpu.VMEM((ROWS, HALF), F32),
            pltpu.VMEM((ROWS, HALF), BF16),
            pltpu.VMEM((BLOCKS, RANK, BLOCK), F32),
        ),
        in_specs=[HBM] * 3,
        out_specs=[VMEM] * 3,
        scratch_shapes=[
            pltpu.VMEM((ROWS, HALF), BF16),
            pltpu.VMEM((RANK, ROWS), BF16),
            pltpu.SemaphoreType.DMA,
            pltpu.SemaphoreType.DMA((CHUNKS,)),
            pltpu.SemaphoreType.DMA((CHUNKS,)),
        ],
        compiler_params=params(12),
        cost_estimate=pl.CostEstimate(
            flops=2 * ROWS * HALF * RANK, bytes_accessed=6 * ROWS * HALF, transcendentals=0
        ),
        name="compensate_own" if own else "compensate_other",
    )(*operands)


def project_kernel(low, blocks, *refs):
    product, terms = refs[-2:]
    for block in range(BLOCKS):
        cols = slice(block * BLOCK, (block + 1) * BLOCK)
        for term, value in enumerate(three_terms(blocks[block])):
            terms[term * RANK : (term + 1) * RANK, cols] = value
    stacked = lax.dot_general(terms[...], low[...], CONTRACT_LAST, preferred_element_type=F32)
    total = stacked[:RANK] + (stacked[RANK : 2 * RANK] + stacked[2 * RANK :])
    if len(refs) == 3:
        total = total + refs[0][:, :ROWS]
    product[...] = jnp.zeros(product.shape, F32)
    product[:, :ROWS] = total


def project(low, blocks, *before):
    return pl.pallas_call(
        project_kernel,
        out_shape=(pltpu.VMEM((RANK, PAD), F32), pltpu.VMEM((3 * RANK, HALF), BF16)),
        in_specs=[VMEM] * (2 + len(before)),
        out_specs=[VMEM] * 2,
        compiler_params=params(12),
        cost_estimate=pl.CostEstimate(
            flops=6 * ROWS * HALF * RANK, bytes_accessed=2 * ROWS * HALF, transcendentals=0
        ),
        name="project",
    )(pltpu.with_memory_space_constraint(low, pltpu.VMEM), blocks, *before)


def inverse_of_lower(gram):
    shape = (GROUP, 2 * RANK)
    groups = RANK // GROUP
    row = lax.broadcasted_iota(jnp.int32, (RANK, RANK), 0)
    column = lax.broadcasted_iota(jnp.int32, (RANK, RANK), 1)
    whole = jnp.concatenate([gram, (row == column).astype(F32)], axis=1)
    work = [whole[g * GROUP : (g + 1) * GROUP] for g in range(groups)]
    index = lax.broadcasted_iota(jnp.int32, shape, 0)
    scale = [jnp.zeros(shape, F32) for _ in range(groups)]
    inside = range(GROUP)
    for g in range(groups):
        rows = [jnp.broadcast_to(work[g][p : p + 1, :], shape) for p in inside]
        cols = [
            [jnp.broadcast_to(work[i][:, g * GROUP + p : g * GROUP + p + 1], shape) for i in range(g, groups)]
            for p in inside
        ]
        entry = {
            (q, p): jnp.broadcast_to(cols[p][0][q : q + 1, :], shape) for p in inside for q in range(p, GROUP)
        }
        for p in inside:
            reciprocal = 1.0 / entry[p, p]
            scale[g] = jnp.where(index == p, entry[p, p], scale[g])
            for q in range(p + 1, GROUP):
                multiplier = entry[q, p] * reciprocal
                for t in range(q, GROUP):
                    entry[t, q] = entry[t, q] - multiplier * entry[t, p]
                rows[q] = rows[q] - multiplier * rows[p]
                cols[q] = [mine - multiplier * pivot for mine, pivot in zip(cols[q], cols[p])]
            rows[p] = rows[p] * reciprocal
        for i in range(g, groups):
            for p in inside:
                factor = cols[p][i - g]
                if i == g:
                    factor = jnp.where(index > p, factor, 0.0)
                work[i] = work[i] - factor * rows[p]
    return jnp.concatenate([w * lax.rsqrt(d) for w, d in zip(work, scale)])[:, RANK:]


def ortho_terms(weights, terms):
    one, two, three = (terms[t * RANK : (t + 1) * RANK] for t in range(3))
    stack = jnp.concatenate([one, two, one, three, two, one])
    return jnp.concatenate(two_terms(jnp.dot(weights, stack, preferred_element_type=F32)))


def factor_kernel(own_terms, other_terms, inverse, weights, ortho):
    stacked = sum(
        lax.dot_general(terms[...], terms[...], CONTRACT_LAST, preferred_element_type=F32)
        for terms in (own_terms, other_terms)
    )

    def part(left, right):
        return stacked[left * RANK : (left + 1) * RANK, right * RANK : (right + 1) * RANK]

    small = part(0, 2) + part(2, 0) + part(1, 1)
    gram = part(0, 0) + ((part(0, 1) + part(1, 0)) + small)
    lower_inverse = inverse_of_lower(gram)
    inverse[...] = lower_inverse
    one, two, three = (term.astype(F32) for term in three_terms(lower_inverse))
    beside = jnp.concatenate([one, one, two, one, two, three], axis=1).astype(BF16)
    weights[...] = beside
    ortho[...] = ortho_terms(beside, own_terms[:, in_half(0)])


def factor(own_terms, other_terms):
    return pl.pallas_call(
        factor_kernel,
        out_shape=(
            pltpu.VMEM((RANK, RANK), F32),
            pltpu.VMEM((RANK, 6 * RANK), BF16),
            pltpu.VMEM((2 * RANK, WIDTH), BF16),
        ),
        in_specs=[VMEM] * 2,
        out_specs=[VMEM] * 3,
        compiler_params=params(12),
        cost_estimate=pl.CostEstimate(flops=10**9, bytes_accessed=10**7, transcendentals=0),
        name="factor",
    )(own_terms, other_terms)


def apply_kernel(
    own_comp,
    other_comp,
    own,
    pair,
    first,
    second,
    inverse,
    weights,
    first_ortho,
    own_terms,
    other_terms,
    new_errors,
    update,
    new_q,
    error_buf,
    update_buf,
    q_buf,
    error_sems,
    update_sems,
    q_sem,
):
    total = (own[...] + pair[...]) + (first[...] + second[...])
    q_t = jnp.dot(
        inverse[...], total * (1.0 / X), precision=lax.Precision.HIGHEST, preferred_element_type=F32
    )
    q_buf[...] = q_t[:, :ROWS]
    copies = [pltpu.make_async_copy(q_buf, new_q, q_sem)]
    copies[0].start()
    high = q_t.astype(BF16).astype(F32)
    stacked = jnp.concatenate([high, high, q_t - high]).T[:ROWS].astype(BF16)
    for half, (comp, terms) in enumerate(((own_comp, own_terms), (other_comp, other_terms))):
        start = half_start(half == 0)
        for chunk in range(CHUNKS):
            cols, at = in_half(chunk), in_hbm(start, chunk)
            ready = half == 0 and chunk == 0
            ortho = first_ortho[...] if ready else ortho_terms(weights[...], terms[:, cols])
            ortho = jnp.concatenate([ortho, ortho[:RANK]])
            approx = jnp.dot(stacked, ortho, preferred_element_type=F32)
            update_buf[half, :, cols] = approx.astype(BF16)
            update_copy = pltpu.make_async_copy(
                update_buf.at[half, :, cols], update.at[:, at], update_sems.at[half, chunk]
            )
            update_copy.start()
            error_buf[half, :, cols] = comp[:, cols] - approx
            error_copy = pltpu.make_async_copy(
                error_buf.at[half, :, cols], new_errors.at[:, at], error_sems.at[half, chunk]
            )
            error_copy.start()
            copies += [update_copy, error_copy]
    for copy in copies:
        copy.wait()


def apply(own_comp, other_comp, *operands):
    comps = [pltpu.with_memory_space_constraint(a, pltpu.VMEM) for a in (own_comp, other_comp)]
    return pl.pallas_call(
        apply_kernel,
        out_shape=(
            jax.ShapeDtypeStruct((ROWS, FEATURES), F32),
            jax.ShapeDtypeStruct((ROWS, FEATURES), BF16),
            jax.ShapeDtypeStruct((RANK, ROWS), F32),
        ),
        in_specs=[VMEM] * (2 + len(operands)),
        out_specs=[HBM] * 3,
        scratch_shapes=[
            pltpu.VMEM((C, ROWS, HALF), F32),
            pltpu.VMEM((C, ROWS, HALF), BF16),
            pltpu.VMEM((RANK, ROWS), F32),
            pltpu.SemaphoreType.DMA((C, CHUNKS)),
            pltpu.SemaphoreType.DMA((C, CHUNKS)),
            pltpu.SemaphoreType.DMA,
        ],
        compiler_params=params(20),
        name="apply",
    )(*comps, *operands)


def send(array, axis, targets):
    return lax.ppermute(array, axis, list(enumerate(targets)))


def add_up(blocks):
    terms = [blocks[i] for i in range(blocks.shape[0])]
    while len(terms) > 1:
        terms = [left + right for left, right in zip(terms[::2], terms[1::2])]
    return terms[0]


def repeat(block, times):
    return jnp.broadcast_to(block, (times,) + block.shape)


def reduce_and_gather(mine):
    block = add_up(lax.all_to_all(mine, ("x", "y"), 0, 0))
    block = add_up(lax.all_to_all(repeat(block, Z), ("z", "c"), 0, 0, axis_index_groups=OWNERS))
    return lax.all_to_all(repeat(block, BLOCKS), ("x", "y"), 0, 0)


def shards(grads, errors, q_start):
    q_t = q_start.T
    other_comp, other_low, other = compensate(grads[0], errors[0], q_t, False)
    received = send(other, "c", SWAP)
    own_comp, own_low, mine = compensate(grads[0], errors[0], q_t, True)
    mine = reduce_and_gather(mine + received)
    other = send(mine, "c", SWAP)
    product, own_terms = project(own_low, mine)
    product, other_terms = project(other_low, other, product)
    pair, first, second = (send(product, "x", targets) for targets in REPLICAS)
    factors = factor(own_terms, other_terms)
    new_errors, update, new_q = apply(
        own_comp, other_comp, product, pair, first, second, *factors, own_terms, other_terms
    )
    return (update, new_errors[None], new_q.T)


def solution(mesh):
    split = Mesh(mesh.devices.reshape(X, Y, Z, C), ("x", "y", "z", "c"))
    rows = ("y", "z", "c")
    return jax.shard_map(
        shards,
        mesh=split,
        in_specs=(P("x", rows, None), P("x", rows, None), P(rows, None)),
        out_specs=(P(rows, None), P("x", rows, None), P(rows, None)),
        check_vma=False,
    )
```

```python
import functools

import jax
import jax.numpy as jnp
from jax import lax
from jax.experimental import pallas as pl
from jax.experimental.pallas import tpu as pltpu
from jax.sharding import Mesh
from jax.sharding import PartitionSpec as P

X, Y, Z, C = 4, 4, 8, 2
RANK = 32
ROWS = 224
PAD = 256
FEATURES = 4096
HALF = FEATURES // C
BLOCKS = X * Y
BLOCK = HALF // BLOCKS
CHUNKS = 2
WIDTH = HALF // CHUNKS
PARTS = ((0, 512), (512, HALF))
GROUP = 8
SWAP = (1, 0)
REPLICAS = ((1, 0, 3, 2), (2, 3, 0, 1), (3, 2, 1, 0))
OWNERS = [[C * z + (half + z // (Z // C)) % C for z in range(Z)] for half in range(C)]
F32, BF16 = jnp.float32, jnp.bfloat16
CONTRACT_LAST = (((1,), (1,)), ((), ()))
VMEM = pl.BlockSpec(memory_space=pltpu.VMEM)
HBM = pl.BlockSpec(memory_space=pltpu.HBM)


def half_start(own):
    half = lax.rem(lax.axis_index("c") + lax.div(lax.axis_index("z"), Z // C), C)
    return (half if own else 1 - half) * HALF


def in_hbm(start, chunk):
    return pl.ds(pl.multiple_of(start + chunk * WIDTH, WIDTH), WIDTH)


def in_half(chunk):
    return slice(chunk * WIDTH, (chunk + 1) * WIDTH)


def params(mebibytes):
    return pltpu.CompilerParams(vmem_limit_bytes=mebibytes * 2**20)


def two_terms(value):
    high = value.astype(BF16)
    return high, (value - high.astype(F32)).astype(BF16)


def three_terms(value):
    high = value.astype(BF16)
    rest = value - high.astype(F32)
    middle = rest.astype(BF16)
    return high, middle, (rest - middle.astype(F32)).astype(BF16)


def compensate_kernel(
    own, grads, errors, q_hbm, comp, low, partial, grad_buf, q_t, q_sem, grad_sems, error_sems
):
    start = half_start(own)
    q_copy = pltpu.make_async_copy(q_hbm, q_t, q_sem)
    q_copy.start()
    copies = []
    for chunk in range(CHUNKS):
        at, cols = in_hbm(start, chunk), in_half(chunk)
        pair = (
            pltpu.make_async_copy(grads.at[:, at], grad_buf.at[:, cols], grad_sems.at[chunk]),
            pltpu.make_async_copy(errors.at[:, at], comp.at[:, cols], error_sems.at[chunk]),
        )
        for copy in pair:
            copy.start()
        copies.append(pair)
    q_copy.wait()
    factor = q_t[...]
    for chunk in range(CHUNKS):
        for copy in copies[chunk]:
            copy.wait()
        cols = in_half(chunk)
        total = grad_buf[:, cols].astype(F32) + comp[:, cols]
        comp[:, cols] = total
        rounded = total.astype(BF16)
        low[:, cols] = rounded
        product = jnp.dot(factor, rounded, preferred_element_type=F32)
        for part in range(WIDTH // BLOCK):
            partial[chunk * (WIDTH // BLOCK) + part] = product[:, part * BLOCK : (part + 1) * BLOCK]


def compensate(grads, errors, q_t, own):
    operands = [pltpu.with_memory_space_constraint(a, pltpu.HBM) for a in (grads, errors, q_t)]
    return pl.pallas_call(
        functools.partial(compensate_kernel, own),
        out_shape=(
            pltpu.VMEM((ROWS, HALF), F32),
            pltpu.VMEM((ROWS, HALF), BF16),
            pltpu.VMEM((BLOCKS, RANK, BLOCK), F32),
        ),
        in_specs=[HBM] * 3,
        out_specs=[VMEM] * 3,
        scratch_shapes=[
            pltpu.VMEM((ROWS, HALF), BF16),
            pltpu.VMEM((RANK, ROWS), BF16),
            pltpu.SemaphoreType.DMA,
            pltpu.SemaphoreType.DMA((CHUNKS,)),
            pltpu.SemaphoreType.DMA((CHUNKS,)),
        ],
        compiler_params=params(12),
        cost_estimate=pl.CostEstimate(
            flops=2 * ROWS * HALF * RANK, bytes_accessed=6 * ROWS * HALF, transcendentals=0
        ),
        name="compensate_own" if own else "compensate_other",
    )(*operands)


def project_kernel(low, blocks, *refs):
    product, terms = refs[-2:]
    for block in range(BLOCKS):
        cols = slice(block * BLOCK, (block + 1) * BLOCK)
        for term, value in enumerate(three_terms(blocks[block])):
            terms[term * RANK : (term + 1) * RANK, cols] = value
    stacked = lax.dot_general(terms[...], low[...], CONTRACT_LAST, preferred_element_type=F32)
    total = stacked[:RANK] + (stacked[RANK : 2 * RANK] + stacked[2 * RANK :])
    if len(refs) == 3:
        total = total + refs[0][:, :ROWS]
    product[...] = jnp.zeros(product.shape, F32)
    product[:, :ROWS] = total


def project(low, blocks, *before):
    return pl.pallas_call(
        project_kernel,
        out_shape=(pltpu.VMEM((RANK, PAD), F32), pltpu.VMEM((3 * RANK, HALF), BF16)),
        in_specs=[VMEM] * (2 + len(before)),
        out_specs=[VMEM] * 2,
        compiler_params=params(12),
        cost_estimate=pl.CostEstimate(
            flops=6 * ROWS * HALF * RANK, bytes_accessed=2 * ROWS * HALF, transcendentals=0
        ),
        name="project",
    )(pltpu.with_memory_space_constraint(low, pltpu.VMEM), blocks, *before)


def inverse_of_lower(gram):
    shape = (GROUP, 2 * RANK)
    groups = RANK // GROUP
    row = lax.broadcasted_iota(jnp.int32, (RANK, RANK), 0)
    column = lax.broadcasted_iota(jnp.int32, (RANK, RANK), 1)
    whole = jnp.concatenate([gram, (row == column).astype(F32)], axis=1)
    work = [whole[g * GROUP : (g + 1) * GROUP] for g in range(groups)]
    index = lax.broadcasted_iota(jnp.int32, shape, 0)
    scale = [jnp.zeros(shape, F32) for _ in range(groups)]
    inside = range(GROUP)
    for g in range(groups):
        rows = [jnp.broadcast_to(work[g][p : p + 1, :], shape) for p in inside]
        cols = [
            [jnp.broadcast_to(work[i][:, g * GROUP + p : g * GROUP + p + 1], shape) for i in range(g, groups)]
            for p in inside
        ]
        entry = {
            (q, p): jnp.broadcast_to(cols[p][0][q : q + 1, :], shape) for p in inside for q in range(p, GROUP)
        }
        for p in inside:
            reciprocal = 1.0 / entry[p, p]
            scale[g] = jnp.where(index == p, entry[p, p], scale[g])
            for q in range(p + 1, GROUP):
                multiplier = entry[q, p] * reciprocal
                for t in range(q, GROUP):
                    entry[t, q] = entry[t, q] - multiplier * entry[t, p]
                rows[q] = rows[q] - multiplier * rows[p]
                cols[q] = [mine - multiplier * pivot for mine, pivot in zip(cols[q], cols[p])]
            rows[p] = rows[p] * reciprocal
        for i in range(g, groups):
            for p in inside:
                factor = cols[p][i - g]
                if i == g:
                    factor = jnp.where(index > p, factor, 0.0)
                work[i] = work[i] - factor * rows[p]
    return jnp.concatenate([w * lax.rsqrt(d) for w, d in zip(work, scale)])[:, RANK:]


def ortho_terms(weights, terms):
    one, two, three = (terms[t * RANK : (t + 1) * RANK] for t in range(3))
    stack = jnp.concatenate([one, two, one, three, two, one])
    return jnp.concatenate(two_terms(jnp.dot(weights, stack, preferred_element_type=F32)))


def factor_kernel(own_terms, other_terms, inverse, weights, ortho):
    stacked = sum(
        lax.dot_general(terms[...], terms[...], CONTRACT_LAST, preferred_element_type=F32)
        for terms in (own_terms, other_terms)
    )

    def part(left, right):
        return stacked[left * RANK : (left + 1) * RANK, right * RANK : (right + 1) * RANK]

    small = part(0, 2) + part(2, 0) + part(1, 1)
    gram = part(0, 0) + ((part(0, 1) + part(1, 0)) + small)
    lower_inverse = inverse_of_lower(gram)
    inverse[...] = lower_inverse
    one, two, three = (term.astype(F32) for term in three_terms(lower_inverse))
    beside = jnp.concatenate([one, one, two, one, two, three], axis=1).astype(BF16)
    weights[...] = beside
    ortho[...] = ortho_terms(beside, own_terms[:, slice(*PARTS[0])])


def factor(own_terms, other_terms):
    return pl.pallas_call(
        factor_kernel,
        out_shape=(
            pltpu.VMEM((RANK, RANK), F32),
            pltpu.VMEM((RANK, 6 * RANK), BF16),
            pltpu.VMEM((2 * RANK, PARTS[0][1]), BF16),
        ),
        in_specs=[VMEM] * 2,
        out_specs=[VMEM] * 3,
        compiler_params=params(12),
        cost_estimate=pl.CostEstimate(flops=10**9, bytes_accessed=10**7, transcendentals=0),
        name="factor",
    )(own_terms, other_terms)


def apply_kernel(
    own_comp,
    other_comp,
    own,
    pair,
    first,
    second,
    inverse,
    weights,
    first_ortho,
    own_terms,
    other_terms,
    new_errors,
    update,
    new_q,
    error_buf,
    update_buf,
    q_buf,
    error_sems,
    update_sems,
    q_sem,
):
    total = (own[...] + pair[...]) + (first[...] + second[...])
    q_t = jnp.dot(
        inverse[...], total * (1.0 / X), precision=lax.Precision.HIGHEST, preferred_element_type=F32
    )
    q_buf[...] = q_t[:, :ROWS]
    copies = [pltpu.make_async_copy(q_buf, new_q, q_sem)]
    copies[0].start()
    high = q_t.astype(BF16).astype(F32)
    stacked = jnp.concatenate([high, high, q_t - high]).T[:ROWS].astype(BF16)
    for half, (comp, terms) in enumerate(((own_comp, own_terms), (other_comp, other_terms))):
        start = half_start(half == 0)
        for chunk, (begin, end) in enumerate(PARTS):
            cols = slice(begin, end)
            at = pl.ds(pl.multiple_of(start + begin, PARTS[0][1]), end - begin)
            ready = half == 0 and chunk == 0
            ortho = first_ortho[...] if ready else ortho_terms(weights[...], terms[:, cols])
            ortho = jnp.concatenate([ortho, ortho[:RANK]])
            approx = jnp.dot(stacked, ortho, preferred_element_type=F32)
            update_buf[half, :, cols] = approx.astype(BF16)
            update_copy = pltpu.make_async_copy(
                update_buf.at[half, :, cols], update.at[:, at], update_sems.at[half, chunk]
            )
            update_copy.start()
            error_buf[half, :, cols] = comp[:, cols] - approx
            error_copy = pltpu.make_async_copy(
                error_buf.at[half, :, cols], new_errors.at[:, at], error_sems.at[half, chunk]
            )
            error_copy.start()
            copies += [update_copy, error_copy]
    for copy in copies:
        copy.wait()


def apply(own_comp, other_comp, *operands):
    comps = [pltpu.with_memory_space_constraint(a, pltpu.VMEM) for a in (own_comp, other_comp)]
    return pl.pallas_call(
        apply_kernel,
        out_shape=(
            jax.ShapeDtypeStruct((ROWS, FEATURES), F32),
            jax.ShapeDtypeStruct((ROWS, FEATURES), BF16),
            jax.ShapeDtypeStruct((RANK, ROWS), F32),
        ),
        in_specs=[VMEM] * (2 + len(operands)),
        out_specs=[HBM] * 3,
        scratch_shapes=[
            pltpu.VMEM((C, ROWS, HALF), F32),
            pltpu.VMEM((C, ROWS, HALF), BF16),
            pltpu.VMEM((RANK, ROWS), F32),
            pltpu.SemaphoreType.DMA((C, len(PARTS))),
            pltpu.SemaphoreType.DMA((C, len(PARTS))),
            pltpu.SemaphoreType.DMA,
        ],
        compiler_params=params(20),
        name="apply",
    )(*comps, *operands)


def send(array, axis, targets):
    return lax.ppermute(array, axis, list(enumerate(targets)))


def add_up(blocks):
    terms = [blocks[i] for i in range(blocks.shape[0])]
    while len(terms) > 1:
        terms = [left + right for left, right in zip(terms[::2], terms[1::2])]
    return terms[0]


def repeat(block, times):
    return jnp.broadcast_to(block, (times,) + block.shape)


def reduce_and_gather(mine):
    block = add_up(lax.all_to_all(mine, ("x", "y"), 0, 0))
    block = add_up(lax.all_to_all(repeat(block, Z), ("z", "c"), 0, 0, axis_index_groups=OWNERS))
    return lax.all_to_all(repeat(block, BLOCKS), ("x", "y"), 0, 0)


def shards(grads, errors, q_start):
    q_t = q_start.T
    other_comp, other_low, other = compensate(grads[0], errors[0], q_t, False)
    received = send(other, "c", SWAP)
    own_comp, own_low, mine = compensate(grads[0], errors[0], q_t, True)
    mine = reduce_and_gather(mine + received)
    other = send(mine, "c", SWAP)
    product, own_terms = project(own_low, mine)
    product, other_terms = project(other_low, other, product)
    pair, first, second = (send(product, "x", targets) for targets in REPLICAS)
    factors = factor(own_terms, other_terms)
    new_errors, update, new_q = apply(
        own_comp, other_comp, product, pair, first, second, *factors, own_terms, other_terms
    )
    return (update, new_errors[None], new_q.T)


def solution(mesh):
    split = Mesh(mesh.devices.reshape(X, Y, Z, C), ("x", "y", "z", "c"))
    rows = ("y", "z", "c")
    return jax.shard_map(
        shards,
        mesh=split,
        in_specs=(P("x", rows, None), P("x", rows, None), P(rows, None)),
        out_specs=(P(rows, None), P("x", rows, None), P(rows, None)),
        check_vma=False,
    )
```

```python
import functools

import jax
import jax.numpy as jnp
from jax import lax
from jax.experimental import pallas as pl
from jax.experimental.pallas import tpu as pltpu
from jax.sharding import Mesh
from jax.sharding import PartitionSpec as P

X, Y, Z, C = 4, 4, 8, 2
RANK = 32
ROWS = 224
PAD = 256
FEATURES = 4096
HALF = FEATURES // C
BLOCKS = X * Y
BLOCK = HALF // BLOCKS
CHUNKS = 2
WIDTH = HALF // CHUNKS
GROUP = 8
SWAP = (1, 0)
REPLICAS = (
    ((1, 0, 3, 2), (2, 0, 3, 1)),
    ((3, 2, 0, 1), (3, 2, 1, 0)),
    ((2, 3, 1, 0), (1, 3, 0, 2)),
)
OWNERS = [[C * z + (half + z // (Z // C)) % C for z in range(Z)] for half in range(C)]
F32, BF16 = jnp.float32, jnp.bfloat16
CONTRACT_LAST = (((1,), (1,)), ((), ()))
VMEM = pl.BlockSpec(memory_space=pltpu.VMEM)
HBM = pl.BlockSpec(memory_space=pltpu.HBM)


def half_start(own):
    half = lax.rem(lax.axis_index("c") + lax.div(lax.axis_index("z"), Z // C), C)
    return (half if own else 1 - half) * HALF


def in_hbm(start, chunk):
    return pl.ds(pl.multiple_of(start + chunk * WIDTH, WIDTH), WIDTH)


def in_half(chunk):
    return slice(chunk * WIDTH, (chunk + 1) * WIDTH)


def params(mebibytes):
    return pltpu.CompilerParams(vmem_limit_bytes=mebibytes * 2**20)


def two_terms(value):
    high = value.astype(BF16)
    return high, (value - high.astype(F32)).astype(BF16)


def three_terms(value):
    high = value.astype(BF16)
    rest = value - high.astype(F32)
    middle = rest.astype(BF16)
    return high, middle, (rest - middle.astype(F32)).astype(BF16)


def compensate_kernel(
    own, grads, errors, q_hbm, comp, low, partial, grad_buf, q_t, q_sem, grad_sems, error_sems
):
    start = half_start(own)
    q_copy = pltpu.make_async_copy(q_hbm, q_t, q_sem)
    q_copy.start()
    copies = []
    for chunk in range(CHUNKS):
        at, cols = in_hbm(start, chunk), in_half(chunk)
        pair = (
            pltpu.make_async_copy(grads.at[:, at], grad_buf.at[:, cols], grad_sems.at[chunk]),
            pltpu.make_async_copy(errors.at[:, at], comp.at[:, cols], error_sems.at[chunk]),
        )
        for copy in pair:
            copy.start()
        copies.append(pair)
    q_copy.wait()
    factor = q_t[...]
    for chunk in range(CHUNKS):
        for copy in copies[chunk]:
            copy.wait()
        cols = in_half(chunk)
        total = grad_buf[:, cols].astype(F32) + comp[:, cols]
        comp[:, cols] = total
        rounded = total.astype(BF16)
        low[:, cols] = rounded
        product = jnp.dot(factor, rounded, preferred_element_type=F32)
        for part in range(WIDTH // BLOCK):
            partial[chunk * (WIDTH // BLOCK) + part] = product[:, part * BLOCK : (part + 1) * BLOCK]


def compensate(grads, errors, q_t, own):
    operands = [pltpu.with_memory_space_constraint(a, pltpu.HBM) for a in (grads, errors, q_t)]
    return pl.pallas_call(
        functools.partial(compensate_kernel, own),
        out_shape=(
            pltpu.VMEM((ROWS, HALF), F32),
            pltpu.VMEM((ROWS, HALF), BF16),
            pltpu.VMEM((BLOCKS, RANK, BLOCK), F32),
        ),
        in_specs=[HBM] * 3,
        out_specs=[VMEM] * 3,
        scratch_shapes=[
            pltpu.VMEM((ROWS, HALF), BF16),
            pltpu.VMEM((RANK, ROWS), BF16),
            pltpu.SemaphoreType.DMA,
            pltpu.SemaphoreType.DMA((CHUNKS,)),
            pltpu.SemaphoreType.DMA((CHUNKS,)),
        ],
        compiler_params=params(12),
        cost_estimate=pl.CostEstimate(
            flops=2 * ROWS * HALF * RANK, bytes_accessed=6 * ROWS * HALF, transcendentals=0
        ),
        name="compensate_own" if own else "compensate_other",
    )(*operands)


def project_kernel(low, blocks, *refs):
    product, terms = refs[-2:]
    for block in range(BLOCKS):
        cols = slice(block * BLOCK, (block + 1) * BLOCK)
        for term, value in enumerate(three_terms(blocks[block])):
            terms[term * RANK : (term + 1) * RANK, cols] = value
    stacked = lax.dot_general(terms[...], low[...], CONTRACT_LAST, preferred_element_type=F32)
    total = stacked[:RANK] + (stacked[RANK : 2 * RANK] + stacked[2 * RANK :])
    if len(refs) == 3:
        total = total + refs[0][:, :ROWS]
    product[...] = jnp.zeros(product.shape, F32)
    product[:, :ROWS] = total


def project(low, blocks, *before):
    return pl.pallas_call(
        project_kernel,
        out_shape=(pltpu.VMEM((RANK, PAD), F32), pltpu.VMEM((3 * RANK, HALF), BF16)),
        in_specs=[VMEM] * (2 + len(before)),
        out_specs=[VMEM] * 2,
        compiler_params=params(12),
        cost_estimate=pl.CostEstimate(
            flops=6 * ROWS * HALF * RANK, bytes_accessed=2 * ROWS * HALF, transcendentals=0
        ),
        name="project",
    )(pltpu.with_memory_space_constraint(low, pltpu.VMEM), blocks, *before)


def inverse_of_lower(gram):
    shape = (GROUP, 2 * RANK)
    groups = RANK // GROUP
    row = lax.broadcasted_iota(jnp.int32, (RANK, RANK), 0)
    column = lax.broadcasted_iota(jnp.int32, (RANK, RANK), 1)
    whole = jnp.concatenate([gram, (row == column).astype(F32)], axis=1)
    work = [whole[g * GROUP : (g + 1) * GROUP] for g in range(groups)]
    index = lax.broadcasted_iota(jnp.int32, shape, 0)
    scale = [jnp.zeros(shape, F32) for _ in range(groups)]
    inside = range(GROUP)
    for g in range(groups):
        rows = [jnp.broadcast_to(work[g][p : p + 1, :], shape) for p in inside]
        cols = [
            [jnp.broadcast_to(work[i][:, g * GROUP + p : g * GROUP + p + 1], shape) for i in range(g, groups)]
            for p in inside
        ]
        entry = {
            (q, p): jnp.broadcast_to(cols[p][0][q : q + 1, :], shape) for p in inside for q in range(p, GROUP)
        }
        for p in inside:
            reciprocal = 1.0 / entry[p, p]
            scale[g] = jnp.where(index == p, entry[p, p], scale[g])
            for q in range(p + 1, GROUP):
                multiplier = entry[q, p] * reciprocal
                for t in range(q, GROUP):
                    entry[t, q] = entry[t, q] - multiplier * entry[t, p]
                rows[q] = rows[q] - multiplier * rows[p]
                cols[q] = [mine - multiplier * pivot for mine, pivot in zip(cols[q], cols[p])]
            rows[p] = rows[p] * reciprocal
        for i in range(g, groups):
            for p in inside:
                factor = cols[p][i - g]
                if i == g:
                    factor = jnp.where(index > p, factor, 0.0)
                work[i] = work[i] - factor * rows[p]
    return jnp.concatenate([w * lax.rsqrt(d) for w, d in zip(work, scale)])[:, RANK:]


def ortho_terms(weights, terms):
    one, two, three = (terms[t * RANK : (t + 1) * RANK] for t in range(3))
    stack = jnp.concatenate([one, two, one, three, two, one])
    return jnp.concatenate(two_terms(jnp.dot(weights, stack, preferred_element_type=F32)))


def factor_kernel(own_terms, other_terms, inverse, weights, ortho):
    stacked = sum(
        lax.dot_general(terms[...], terms[...], CONTRACT_LAST, preferred_element_type=F32)
        for terms in (own_terms, other_terms)
    )

    def part(left, right):
        return stacked[left * RANK : (left + 1) * RANK, right * RANK : (right + 1) * RANK]

    small = part(0, 2) + part(2, 0) + part(1, 1)
    gram = part(0, 0) + ((part(0, 1) + part(1, 0)) + small)
    lower_inverse = inverse_of_lower(gram)
    inverse[...] = lower_inverse
    one, two, three = (term.astype(F32) for term in three_terms(lower_inverse))
    beside = jnp.concatenate([one, one, two, one, two, three], axis=1).astype(BF16)
    weights[...] = beside
    ortho[...] = ortho_terms(beside, own_terms[:, in_half(0)])


def factor(own_terms, other_terms):
    return pl.pallas_call(
        factor_kernel,
        out_shape=(
            pltpu.VMEM((RANK, RANK), F32),
            pltpu.VMEM((RANK, 6 * RANK), BF16),
            pltpu.VMEM((2 * RANK, WIDTH), BF16),
        ),
        in_specs=[VMEM] * 2,
        out_specs=[VMEM] * 3,
        compiler_params=params(12),
        cost_estimate=pl.CostEstimate(flops=10**9, bytes_accessed=10**7, transcendentals=0),
        name="factor",
    )(own_terms, other_terms)


def apply_kernel(
    own_comp,
    other_comp,
    own,
    pair,
    first,
    second,
    inverse,
    weights,
    first_ortho,
    own_terms,
    other_terms,
    new_errors,
    update,
    new_q,
    error_buf,
    update_buf,
    q_buf,
    error_sems,
    update_sems,
    q_sem,
):
    swapped = lax.axis_index("c") == 0
    one, two = pair[...], first[...]
    total = (own[...] + jnp.where(swapped, one, two)) + (jnp.where(swapped, two, one) + second[...])
    q_t = jnp.dot(
        inverse[...], total * (1.0 / X), precision=lax.Precision.HIGHEST, preferred_element_type=F32
    )
    q_buf[...] = q_t[:, :ROWS]
    copies = [pltpu.make_async_copy(q_buf, new_q, q_sem)]
    copies[0].start()
    high = q_t.astype(BF16).astype(F32)
    stacked = jnp.concatenate([high, high, q_t - high]).T[:ROWS].astype(BF16)
    for half, (comp, terms) in enumerate(((own_comp, own_terms), (other_comp, other_terms))):
        start = half_start(half == 0)
        for chunk in range(CHUNKS):
            cols, at = in_half(chunk), in_hbm(start, chunk)
            ready = half == 0 and chunk == 0
            ortho = first_ortho[...] if ready else ortho_terms(weights[...], terms[:, cols])
            ortho = jnp.concatenate([ortho, ortho[:RANK]])
            approx = jnp.dot(stacked, ortho, preferred_element_type=F32)
            update_buf[half, :, cols] = approx.astype(BF16)
            update_copy = pltpu.make_async_copy(
                update_buf.at[half, :, cols], update.at[:, at], update_sems.at[half, chunk]
            )
            update_copy.start()
            error_buf[half, :, cols] = comp[:, cols] - approx
            error_copy = pltpu.make_async_copy(
                error_buf.at[half, :, cols], new_errors.at[:, at], error_sems.at[half, chunk]
            )
            error_copy.start()
            copies += [update_copy, error_copy]
    for copy in copies:
        copy.wait()


def apply(own_comp, other_comp, *operands):
    comps = [pltpu.with_memory_space_constraint(a, pltpu.VMEM) for a in (own_comp, other_comp)]
    return pl.pallas_call(
        apply_kernel,
        out_shape=(
            jax.ShapeDtypeStruct((ROWS, FEATURES), F32),
            jax.ShapeDtypeStruct((ROWS, FEATURES), BF16),
            jax.ShapeDtypeStruct((RANK, ROWS), F32),
        ),
        in_specs=[VMEM] * (2 + len(operands)),
        out_specs=[HBM] * 3,
        scratch_shapes=[
            pltpu.VMEM((C, ROWS, HALF), F32),
            pltpu.VMEM((C, ROWS, HALF), BF16),
            pltpu.VMEM((RANK, ROWS), F32),
            pltpu.SemaphoreType.DMA((C, CHUNKS)),
            pltpu.SemaphoreType.DMA((C, CHUNKS)),
            pltpu.SemaphoreType.DMA,
        ],
        compiler_params=params(20),
        name="apply",
    )(*comps, *operands)


def send(array, axis, targets):
    return lax.ppermute(array, axis, list(enumerate(targets)))


def add_up(blocks):
    terms = [blocks[i] for i in range(blocks.shape[0])]
    while len(terms) > 1:
        terms = [left + right for left, right in zip(terms[::2], terms[1::2])]
    return terms[0]


def send_by_core(array, targets):
    pairs = [(C * x + c, C * targets[c][x] + c) for x in range(X) for c in range(C)]
    return lax.ppermute(array, ("x", "c"), pairs)


def repeat(block, times):
    return jnp.broadcast_to(block, (times,) + block.shape)


def reduce_and_gather(mine):
    block = add_up(lax.all_to_all(mine, ("x", "y"), 0, 0))
    block = add_up(lax.all_to_all(repeat(block, Z), ("z", "c"), 0, 0, axis_index_groups=OWNERS))
    return lax.all_to_all(repeat(block, BLOCKS), ("x", "y"), 0, 0)


def shards(grads, errors, q_start):
    q_t = q_start.T
    other_comp, other_low, other = compensate(grads[0], errors[0], q_t, False)
    received = send(other, "c", SWAP)
    own_comp, own_low, mine = compensate(grads[0], errors[0], q_t, True)
    mine = reduce_and_gather(mine + received)
    other = send(mine, "c", SWAP)
    product, own_terms = project(own_low, mine)
    product, other_terms = project(other_low, other, product)
    pair, first, second = (send_by_core(product, targets) for targets in REPLICAS)
    factors = factor(own_terms, other_terms)
    new_errors, update, new_q = apply(
        own_comp, other_comp, product, pair, first, second, *factors, own_terms, other_terms
    )
    return (update, new_errors[None], new_q.T)


def solution(mesh):
    split = Mesh(mesh.devices.reshape(X, Y, Z, C), ("x", "y", "z", "c"))
    rows = ("y", "z", "c")
    return jax.shard_map(
        shards,
        mesh=split,
        in_specs=(P("x", rows, None), P("x", rows, None), P(rows, None)),
        out_specs=(P(rows, None), P("x", rows, None), P(rows, None)),
        check_vma=False,
    )
```

```python
import functools

import jax
import jax.numpy as jnp
from jax import lax
from jax.experimental import pallas as pl
from jax.experimental.pallas import tpu as pltpu
from jax.sharding import Mesh
from jax.sharding import PartitionSpec as P

X, Y, Z, C = 4, 4, 8, 2
RANK = 32
ROWS = 224
PAD = 256
FEATURES = 4096
HALF = FEATURES // C
BLOCKS = X * Y
BLOCK = HALF // BLOCKS
CHUNKS = 2
WIDTH = HALF // CHUNKS
PARTS = ((0, 512), (512, HALF))
GROUP = 8
SWAP = (1, 0)
REPLICAS = (
    ((1, 0, 3, 2), (2, 0, 3, 1)),
    ((3, 2, 0, 1), (3, 2, 1, 0)),
    ((2, 3, 1, 0), (1, 3, 0, 2)),
)
OWNERS = [[C * z + (half + z // (Z // C)) % C for z in range(Z)] for half in range(C)]
F32, BF16 = jnp.float32, jnp.bfloat16
CONTRACT_LAST = (((1,), (1,)), ((), ()))
VMEM = pl.BlockSpec(memory_space=pltpu.VMEM)
HBM = pl.BlockSpec(memory_space=pltpu.HBM)


def half_start(own):
    half = lax.rem(lax.axis_index("c") + lax.div(lax.axis_index("z"), Z // C), C)
    return (half if own else 1 - half) * HALF


def in_hbm(start, chunk):
    return pl.ds(pl.multiple_of(start + chunk * WIDTH, WIDTH), WIDTH)


def in_half(chunk):
    return slice(chunk * WIDTH, (chunk + 1) * WIDTH)


def params(mebibytes):
    return pltpu.CompilerParams(vmem_limit_bytes=mebibytes * 2**20)


def two_terms(value):
    high = value.astype(BF16)
    return high, (value - high.astype(F32)).astype(BF16)


def three_terms(value):
    high = value.astype(BF16)
    rest = value - high.astype(F32)
    middle = rest.astype(BF16)
    return high, middle, (rest - middle.astype(F32)).astype(BF16)


def compensate_kernel(
    own, grads, errors, q_hbm, comp, low, partial, grad_buf, q_t, q_sem, grad_sems, error_sems
):
    start = half_start(own)
    q_copy = pltpu.make_async_copy(q_hbm, q_t, q_sem)
    q_copy.start()
    copies = []
    for chunk in range(CHUNKS):
        at, cols = in_hbm(start, chunk), in_half(chunk)
        pair = (
            pltpu.make_async_copy(grads.at[:, at], grad_buf.at[:, cols], grad_sems.at[chunk]),
            pltpu.make_async_copy(errors.at[:, at], comp.at[:, cols], error_sems.at[chunk]),
        )
        for copy in pair:
            copy.start()
        copies.append(pair)
    q_copy.wait()
    factor = q_t[...]
    for chunk in range(CHUNKS):
        for copy in copies[chunk]:
            copy.wait()
        cols = in_half(chunk)
        total = grad_buf[:, cols].astype(F32) + comp[:, cols]
        comp[:, cols] = total
        rounded = total.astype(BF16)
        low[:, cols] = rounded
        product = jnp.dot(factor, rounded, preferred_element_type=F32)
        for part in range(WIDTH // BLOCK):
            partial[chunk * (WIDTH // BLOCK) + part] = product[:, part * BLOCK : (part + 1) * BLOCK]


def compensate(grads, errors, q_t, own):
    operands = [pltpu.with_memory_space_constraint(a, pltpu.HBM) for a in (grads, errors, q_t)]
    return pl.pallas_call(
        functools.partial(compensate_kernel, own),
        out_shape=(
            pltpu.VMEM((ROWS, HALF), F32),
            pltpu.VMEM((ROWS, HALF), BF16),
            pltpu.VMEM((BLOCKS, RANK, BLOCK), F32),
        ),
        in_specs=[HBM] * 3,
        out_specs=[VMEM] * 3,
        scratch_shapes=[
            pltpu.VMEM((ROWS, HALF), BF16),
            pltpu.VMEM((RANK, ROWS), BF16),
            pltpu.SemaphoreType.DMA,
            pltpu.SemaphoreType.DMA((CHUNKS,)),
            pltpu.SemaphoreType.DMA((CHUNKS,)),
        ],
        compiler_params=params(12),
        cost_estimate=pl.CostEstimate(
            flops=2 * ROWS * HALF * RANK, bytes_accessed=6 * ROWS * HALF, transcendentals=0
        ),
        name="compensate_own" if own else "compensate_other",
    )(*operands)


def project_kernel(low, blocks, *refs):
    product, terms = refs[-2:]
    for block in range(BLOCKS):
        cols = slice(block * BLOCK, (block + 1) * BLOCK)
        for term, value in enumerate(three_terms(blocks[block])):
            terms[term * RANK : (term + 1) * RANK, cols] = value
    stacked = lax.dot_general(terms[...], low[...], CONTRACT_LAST, preferred_element_type=F32)
    total = stacked[:RANK] + (stacked[RANK : 2 * RANK] + stacked[2 * RANK :])
    if len(refs) == 3:
        total = total + refs[0][:, :ROWS]
    product[...] = jnp.zeros(product.shape, F32)
    product[:, :ROWS] = total


def project(low, blocks, *before):
    return pl.pallas_call(
        project_kernel,
        out_shape=(pltpu.VMEM((RANK, PAD), F32), pltpu.VMEM((3 * RANK, HALF), BF16)),
        in_specs=[VMEM] * (2 + len(before)),
        out_specs=[VMEM] * 2,
        compiler_params=params(12),
        cost_estimate=pl.CostEstimate(
            flops=6 * ROWS * HALF * RANK, bytes_accessed=2 * ROWS * HALF, transcendentals=0
        ),
        name="project",
    )(pltpu.with_memory_space_constraint(low, pltpu.VMEM), blocks, *before)


def inverse_of_lower(gram):
    shape = (GROUP, 2 * RANK)
    groups = RANK // GROUP
    row = lax.broadcasted_iota(jnp.int32, (RANK, RANK), 0)
    column = lax.broadcasted_iota(jnp.int32, (RANK, RANK), 1)
    whole = jnp.concatenate([gram, (row == column).astype(F32)], axis=1)
    work = [whole[g * GROUP : (g + 1) * GROUP] for g in range(groups)]
    index = lax.broadcasted_iota(jnp.int32, shape, 0)
    scale = [jnp.zeros(shape, F32) for _ in range(groups)]
    inside = range(GROUP)
    for g in range(groups):
        rows = [jnp.broadcast_to(work[g][p : p + 1, :], shape) for p in inside]
        cols = [
            [jnp.broadcast_to(work[i][:, g * GROUP + p : g * GROUP + p + 1], shape) for i in range(g, groups)]
            for p in inside
        ]
        entry = {
            (q, p): jnp.broadcast_to(cols[p][0][q : q + 1, :], shape) for p in inside for q in range(p, GROUP)
        }
        for p in inside:
            reciprocal = 1.0 / entry[p, p]
            scale[g] = jnp.where(index == p, entry[p, p], scale[g])
            for q in range(p + 1, GROUP):
                multiplier = entry[q, p] * reciprocal
                for t in range(q, GROUP):
                    entry[t, q] = entry[t, q] - multiplier * entry[t, p]
                rows[q] = rows[q] - multiplier * rows[p]
                cols[q] = [mine - multiplier * pivot for mine, pivot in zip(cols[q], cols[p])]
            rows[p] = rows[p] * reciprocal
        for i in range(g, groups):
            for p in inside:
                factor = cols[p][i - g]
                if i == g:
                    factor = jnp.where(index > p, factor, 0.0)
                work[i] = work[i] - factor * rows[p]
    return jnp.concatenate([w * lax.rsqrt(d) for w, d in zip(work, scale)])[:, RANK:]


def ortho_terms(weights, terms):
    one, two, three = (terms[t * RANK : (t + 1) * RANK] for t in range(3))
    stack = jnp.concatenate([one, two, one, three, two, one])
    return jnp.concatenate(two_terms(jnp.dot(weights, stack, preferred_element_type=F32)))


def factor_kernel(own_terms, other_terms, inverse, weights, ortho):
    stacked = sum(
        lax.dot_general(terms[...], terms[...], CONTRACT_LAST, preferred_element_type=F32)
        for terms in (own_terms, other_terms)
    )

    def part(left, right):
        return stacked[left * RANK : (left + 1) * RANK, right * RANK : (right + 1) * RANK]

    small = part(0, 2) + part(2, 0) + part(1, 1)
    gram = part(0, 0) + ((part(0, 1) + part(1, 0)) + small)
    lower_inverse = inverse_of_lower(gram)
    inverse[...] = lower_inverse
    one, two, three = (term.astype(F32) for term in three_terms(lower_inverse))
    beside = jnp.concatenate([one, one, two, one, two, three], axis=1).astype(BF16)
    weights[...] = beside
    ortho[...] = ortho_terms(beside, own_terms[:, slice(*PARTS[0])])


def factor(own_terms, other_terms):
    return pl.pallas_call(
        factor_kernel,
        out_shape=(
            pltpu.VMEM((RANK, RANK), F32),
            pltpu.VMEM((RANK, 6 * RANK), BF16),
            pltpu.VMEM((2 * RANK, PARTS[0][1]), BF16),
        ),
        in_specs=[VMEM] * 2,
        out_specs=[VMEM] * 3,
        compiler_params=params(12),
        cost_estimate=pl.CostEstimate(flops=10**9, bytes_accessed=10**7, transcendentals=0),
        name="factor",
    )(own_terms, other_terms)


def apply_kernel(
    own_comp,
    other_comp,
    own,
    pair,
    first,
    second,
    inverse,
    weights,
    first_ortho,
    own_terms,
    other_terms,
    new_errors,
    update,
    new_q,
    error_buf,
    update_buf,
    q_buf,
    error_sems,
    update_sems,
    q_sem,
):
    swapped = lax.axis_index("c") == 0
    one, two = pair[...], first[...]
    total = (own[...] + jnp.where(swapped, one, two)) + (jnp.where(swapped, two, one) + second[...])
    q_t = jnp.dot(
        inverse[...], total * (1.0 / X), precision=lax.Precision.HIGHEST, preferred_element_type=F32
    )
    q_buf[...] = q_t[:, :ROWS]
    copies = [pltpu.make_async_copy(q_buf, new_q, q_sem)]
    copies[0].start()
    high = q_t.astype(BF16).astype(F32)
    stacked = jnp.concatenate([high, high, q_t - high]).T[:ROWS].astype(BF16)
    for half, (comp, terms) in enumerate(((own_comp, own_terms), (other_comp, other_terms))):
        start = half_start(half == 0)
        for chunk, (begin, end) in enumerate(PARTS):
            cols = slice(begin, end)
            at = pl.ds(pl.multiple_of(start + begin, PARTS[0][1]), end - begin)
            ready = half == 0 and chunk == 0
            ortho = first_ortho[...] if ready else ortho_terms(weights[...], terms[:, cols])
            ortho = jnp.concatenate([ortho, ortho[:RANK]])
            approx = jnp.dot(stacked, ortho, preferred_element_type=F32)
            update_buf[half, :, cols] = approx.astype(BF16)
            update_copy = pltpu.make_async_copy(
                update_buf.at[half, :, cols], update.at[:, at], update_sems.at[half, chunk]
            )
            update_copy.start()
            error_buf[half, :, cols] = comp[:, cols] - approx
            error_copy = pltpu.make_async_copy(
                error_buf.at[half, :, cols], new_errors.at[:, at], error_sems.at[half, chunk]
            )
            error_copy.start()
            copies += [update_copy, error_copy]
    for copy in copies:
        copy.wait()


def apply(own_comp, other_comp, *operands):
    comps = [pltpu.with_memory_space_constraint(a, pltpu.VMEM) for a in (own_comp, other_comp)]
    return pl.pallas_call(
        apply_kernel,
        out_shape=(
            jax.ShapeDtypeStruct((ROWS, FEATURES), F32),
            jax.ShapeDtypeStruct((ROWS, FEATURES), BF16),
            jax.ShapeDtypeStruct((RANK, ROWS), F32),
        ),
        in_specs=[VMEM] * (2 + len(operands)),
        out_specs=[HBM] * 3,
        scratch_shapes=[
            pltpu.VMEM((C, ROWS, HALF), F32),
            pltpu.VMEM((C, ROWS, HALF), BF16),
            pltpu.VMEM((RANK, ROWS), F32),
            pltpu.SemaphoreType.DMA((C, len(PARTS))),
            pltpu.SemaphoreType.DMA((C, len(PARTS))),
            pltpu.SemaphoreType.DMA,
        ],
        compiler_params=params(20),
        name="apply",
    )(*comps, *operands)


def send(array, axis, targets):
    return lax.ppermute(array, axis, list(enumerate(targets)))


def add_up(blocks):
    terms = [blocks[i] for i in range(blocks.shape[0])]
    while len(terms) > 1:
        terms = [left + right for left, right in zip(terms[::2], terms[1::2])]
    return terms[0]


def send_by_core(array, targets):
    pairs = [(C * x + c, C * targets[c][x] + c) for x in range(X) for c in range(C)]
    return lax.ppermute(array, ("x", "c"), pairs)


def repeat(block, times):
    return jnp.broadcast_to(block, (times,) + block.shape)


def reduce_and_gather(mine):
    block = add_up(lax.all_to_all(mine, ("x", "y"), 0, 0))
    block = add_up(lax.all_to_all(repeat(block, Z), ("z", "c"), 0, 0, axis_index_groups=OWNERS))
    return lax.all_to_all(repeat(block, BLOCKS), ("x", "y"), 0, 0)


def shards(grads, errors, q_start):
    q_t = q_start.T
    other_comp, other_low, other = compensate(grads[0], errors[0], q_t, False)
    received = send(other, "c", SWAP)
    own_comp, own_low, mine = compensate(grads[0], errors[0], q_t, True)
    mine = reduce_and_gather(mine + received)
    other = send(mine, "c", SWAP)
    product, own_terms = project(own_low, mine)
    product, other_terms = project(other_low, other, product)
    pair, first, second = (send_by_core(product, targets) for targets in REPLICAS)
    factors = factor(own_terms, other_terms)
    new_errors, update, new_q = apply(
        own_comp, other_comp, product, pair, first, second, *factors, own_terms, other_terms
    )
    return (update, new_errors[None], new_q.T)


def solution(mesh):
    split = Mesh(mesh.devices.reshape(X, Y, Z, C), ("x", "y", "z", "c"))
    rows = ("y", "z", "c")
    return jax.shard_map(
        shards,
        mesh=split,
        in_specs=(P("x", rows, None), P("x", rows, None), P(rows, None)),
        out_specs=(P(rows, None), P("x", rows, None), P(rows, None)),
        check_vma=False,
    )
```
